256 devices in a mesh: lat: 32 (over z_lo, y, core), lev: 8 (over x, z_hi).
Axes of the slice: x: 4, y: 4, z: 8 (z_hi: 2, z_lo: 4; z = z_hi * 4 + z_lo), core: 2. Of those that a mesh axis runs over, the one named last changes fastest.
Arguments:
- u_wind: bfloat16 [128, 64, 2880], P('lat', 'lev'), may hold values from -4 to 4
- v_wind: bfloat16 [128, 64, 2880], P('lat', 'lev'), may hold values from -4 to 4
- thickness: float32 [128, 64, 2880], P('lat', 'lev'), may hold values from 0.5 to 2
- tracer: float32 [128, 64, 2880], P('lat', 'lev'), may hold values from -5 to 5
- remap_index: int32 [65], replicated, may hold values from 0 to 63, as said below
- remap_frac: float32 [65], replicated, may hold values from 0 to 1, as said below
Outputs:
- u_filtered: bfloat16 [128, 64, 2880], P('lat', 'lev')
- v_filtered: bfloat16 [128, 64, 2880], P('lat', 'lev')
- thickness_out: float32 [128, 64, 2880], P('lat', None, 'lev')
- tracer_out: float32 [128, 64, 2880], P('lat', None, 'lev')
The draws below stay inside these ranges and needn't reach their ends.
Inputs may be any that keep to these rules, and one draw needn't show every extreme that they name: remap_index[k] is k or k - 1 for 0 < k < 64; remap_index[0] = 0 and remap_index[64] = 63. remap_frac[k] lies in [0, 0.35) where remap_index[k] = k and in (0.65, 1] where remap_index[k] = k - 1; remap_frac[0] = 0 and remap_frac[64] = 1.
All inputs are finite; a program needn't handle non-finite values.
Results may differ from the reference program's by a relative error of at most 0.0028.
Values may be sent and summed in bfloat16 or wider, within the bound.
No kernel may reach another device: no remote copies, remote signals or barrier semaphores. Data moves between devices by JAX's collectives and lax.ppermute only.
A program may use at most 64 MiB of HBM per device.

```python
import math
import jax
import jax.numpy as jnp
import numpy as np
from jax import lax

NLON = 2880
NLAT = 128
NLEV = 64


def interface_offsets(key):
    offsets = jax.random.randint(jax.random.fold_in(key, 11), (NLEV + 1,), 0, 2)
    level_ids = jnp.arange(NLEV + 1, dtype=jnp.int32)
    offsets = jnp.where(level_ids == 0, 0, jnp.where(level_ids == NLEV, 1, offsets))
    return offsets.astype(jnp.int32)


def draw_remap_index(key, part):
    offsets = interface_offsets(key)
    return (jnp.arange(NLEV + 1, dtype=jnp.int32) - offsets).astype(jnp.int32)


def draw_remap_frac(key, part):
    offsets = interface_offsets(key)
    key = jax.random.fold_in(key, 5)
    spread = jax.random.uniform(key, (NLEV + 1,), jnp.float32, 0.0, 0.35)
    fraction = jnp.where(offsets == 1, 1.0 - spread, spread)
    level_ids = jnp.arange(NLEV + 1, dtype=jnp.int32)
    fraction = jnp.where(level_ids == 0, 0.0, jnp.where(level_ids == NLEV, 1.0, fraction))
    return fraction.astype(jnp.float32)


def block_levels(stream_key, extent, pieces, least, high):
    def one(position, parts):
        heights = jax.random.uniform(jax.random.fold_in(jax.random.fold_in(stream_key, 6), position), (parts,), jnp.float32, least / len(pieces), high / len(pieces))
        return jnp.repeat(jnp.exp(heights), extent[position] // parts).reshape((-1,) + (1,) * (len(extent) - position - 1))

    loudness = one(*pieces[0])
    for cut in pieces[1:]:
        loudness = loudness * one(*cut)
    return loudness


def gaussian(stream_key, extent, deviation, limit, cuts=(), held_as=jnp.bfloat16):
    gain = block_levels(stream_key, extent, cuts, -0.22, 0.18) if cuts else 1.0
    entries = jax.random.normal(stream_key, extent, jnp.float32) * deviation * gain
    return jnp.minimum(jnp.maximum(entries, -limit), limit).astype(held_as)


def setup_inputs(seed: int = 0) -> dict:
    keys = jax.random.split(jax.random.key(seed), 7)
    u_wind = gaussian(keys[0], (NLAT, NLEV, NLON), 1.0, 4.0, ((0, 32), (1, 8)))
    v_wind = gaussian(keys[1], (NLAT, NLEV, NLON), 1.0, 4.0, ((0, 32), (1, 8)))
    thickness = jnp.clip(0.5 + 1.5 * jax.random.uniform(keys[2], (NLAT, NLEV, NLON), jnp.float32) ** block_levels(keys[2], (NLAT, NLEV, NLON), ((0, 32), (1, 8)), -0.2, 0.2), 0.5, 2.0)
    tracer = gaussian(keys[3], (NLAT, NLEV, NLON), 1.0, 5.0, ((0, 32), (1, 8)), jnp.float32)
    remap_index = draw_remap_index(jax.random.fold_in(keys[6], 71), 0)
    remap_frac = draw_remap_frac(jax.random.fold_in(keys[6], 71), 0)
    return {"u_wind": u_wind, "v_wind": v_wind, "thickness": thickness, "tracer": tracer, "remap_index": remap_index, "remap_frac": remap_frac}


COS_EDGE = math.cos(66.0 * math.pi / 180.0)


def hartley_table(lon_count):
    block_size = 240 if lon_count % 240 == 0 else lon_count
    columns = jnp.arange(lon_count, dtype=jnp.int32)

    def row_block(first_row):
        row_ids = first_row + jnp.arange(block_size, dtype=jnp.int32)
        phase_index = (row_ids[:, None] * columns[None, :]) % lon_count
        angles = (2.0 * jnp.pi / lon_count) * phase_index.astype(jnp.float32)
        return (jnp.cos(angles) + jnp.sin(angles)).astype(jnp.bfloat16)

    starts = jnp.arange(lon_count // block_size, dtype=jnp.int32) * block_size
    return lax.map(row_block, starts).reshape(lon_count, lon_count)


def latitude_damping(lat_ids, lat_count, lon_count):
    pole_distance = jnp.minimum(lat_ids, lat_count - 1 - lat_ids)
    is_polar = 15 * pole_distance < 2 * (lat_count - 1)
    colatitude = jnp.sin(jnp.pi * pole_distance.astype(jnp.float32) / (lat_count - 1))
    damp_ratio = (colatitude / COS_EDGE) ** 2
    wavenumber = jnp.arange(lon_count, dtype=jnp.int32)
    wave_index = jnp.minimum(wavenumber, lon_count - wavenumber)
    sine_square = jnp.sin(jnp.pi * wave_index.astype(jnp.float32) / lon_count) ** 2
    sine_square = jnp.where(wave_index == 0, 1.0, sine_square)
    damping = jnp.minimum(1.0, damp_ratio[:, None] / sine_square[None, :])
    damping = jnp.where(wave_index[None, :] == 0, 1.0, damping)
    return is_polar, damping


def advect(field, faces_x, faces_y):
    flux_x = jnp.maximum(faces_x, 0.0) * jnp.roll(field, 1, axis=2) + jnp.minimum(faces_x, 0.0) * field
    padded = jnp.pad(field, ((1, 1), (0, 0), (0, 0)))
    flux_y = jnp.maximum(faces_y, 0.0) * padded[:-1] + jnp.minimum(faces_y, 0.0) * padded[1:]
    return field - (jnp.roll(flux_x, -1, axis=2) - flux_x) - (flux_y[1:] - flux_y[:-1])


def interfaces(field, remap_index, remap_frac):
    zeros_row = jnp.zeros((field.shape[0], 1, field.shape[2]), field.dtype)
    cumulative = jnp.concatenate([zeros_row, jnp.cumsum(field, axis=1)], axis=1)
    picked = jnp.take(cumulative, remap_index, axis=1)
    inside = jnp.take(field, remap_index, axis=1)
    return picked + remap_frac[None, :, None] * inside


def reference(u_wind, v_wind, thickness, tracer, remap_index, remap_frac):
    hartley = hartley_table(NLON)
    chosen = np.array([lat_id for lat_id in range(NLAT) if 15 * min(lat_id, NLAT - 1 - lat_id) < 2 * (NLAT - 1)], dtype=np.int32)
    winds = jnp.stack([u_wind, v_wind])
    polar_rows = winds[:, chosen]
    is_polar, damping = latitude_damping(jnp.asarray(chosen, dtype=jnp.int32), NLAT, NLON)
    spectra = jnp.dot(polar_rows.reshape(-1, NLON), hartley, preferred_element_type=jnp.float32)
    spectra = (spectra.reshape(polar_rows.shape) * damping[None, :, None, :]).astype(jnp.bfloat16)
    smooth = jnp.dot(spectra.reshape(-1, NLON), hartley, preferred_element_type=jnp.float32) / NLON
    smooth = smooth.reshape(polar_rows.shape).astype(jnp.bfloat16)
    winds = winds.at[:, chosen].set(smooth)
    courant = jnp.clip(0.05 * winds.astype(jnp.float32), -0.15, 0.15)
    courant_x = courant[0]
    courant_y = courant[1]
    faces_x = 0.5 * (jnp.roll(courant_x, 1, axis=2) + courant_x)
    zeros_row = jnp.zeros((1, NLEV, NLON), jnp.float32)
    faces_y = jnp.concatenate([zeros_row, 0.5 * (courant_y[:-1] + courant_y[1:]), zeros_row], axis=0)
    mass = tracer * thickness
    thick_adv = advect(thickness, faces_x, faces_y)
    mass_adv = advect(mass, faces_x, faces_y)
    level_p = interfaces(thick_adv, remap_index, remap_frac)
    level_m = interfaces(mass_adv, remap_index, remap_frac)
    thickness_out = level_p[:, 1:] - level_p[:, :-1]
    tracer_out = (level_m[:, 1:] - level_m[:, :-1]) / thickness_out
    return winds[0], winds[1], thickness_out, tracer_out
```

```python
import functools
import math

import jax
import jax.numpy as jnp
import ml_dtypes
import numpy as np
from jax import lax
from jax.experimental import pallas as pl
from jax.experimental.pallas import tpu as pltpu
from jax.sharding import PartitionSpec as P

COS_EDGE = math.cos(66.0 * math.pi / 180.0)
LANES = 128
THICK_MID = 1.25


def padded_to(count):
    return -(-count // LANES) * LANES


def filter_parts(lon_count):
    parts = []
    column = 0
    for first, step, points in (
        (1, 2, lon_count // 2),
        (2, 4, lon_count // 4),
        (4, 8, lon_count // 8),
        (0, 8, lon_count // 8),
    ):
        parts.append((first, step, points, column))
        column += padded_to(points)
    return parts, column


def table_places(parts):
    odd, two, four, eight = (padded_to(part[2]) for part in parts)
    return [(0, 0, odd), (0, odd, two), (two, odd, four), (two, odd + four, eight)]


def filter_tables(lat_count, lon_count):
    phase = 2.0 * np.pi * np.arange(lon_count) / lon_count
    rounded = (np.cos(phase) + np.sin(phase)).astype(np.float32).astype(ml_dtypes.bfloat16)
    polar = [d for d in range((lat_count + 1) // 2) if 15 * d < 2 * (lat_count - 1)]
    ratio = (np.sin(np.pi * np.array(polar, np.float64) / (lat_count - 1)) / COS_EDGE) ** 2
    wave = np.arange(lon_count)
    wave = np.minimum(wave, lon_count - wave)
    sine_square = np.sin(np.pi * wave / lon_count) ** 2
    sine_square[0] = 1.0
    values = np.minimum(1.0, ratio[:, None] / sine_square[None, :])
    values[:, 0] = 1.0

    parts, columns = filter_parts(lon_count)
    places = table_places(parts)
    tables = np.zeros((places[0][2], places[0][2] + places[1][2]), ml_dtypes.bfloat16)
    damping = np.zeros((len(polar), 1, columns), np.float32)
    for (first, step, points, column), (row, left, _) in zip(parts, places):
        waves = first + step * np.arange(points)
        tables[row : row + points, left : left + points] = rounded[
            np.arange(points)[:, None] * waves[None, :] % lon_count
        ]
        damping[:, 0, column : column + points] = values[:, waves]
    return tables, damping


def filter_advect(
    lat_count,
    u_ref,
    v_ref,
    thick_ref,
    tracer_ref,
    low_ref,
    high_ref,
    table_ref,
    damp_ref,
    u_out,
    v_out,
    send_ref,
    real_ref,
    work_ref,
    split_ref,
    prod_ref,
    spec_ref,
    edge_ref,
):
    lat_rows, level_rows, lon_count = u_ref.shape
    sectors = send_ref.shape[0]
    sector_wide = send_ref.shape[2]
    sector = lon_count // sectors
    groups, _, padded = real_ref.shape
    distances = damp_ref.shape[0]
    first_lat = lax.axis_index("lat") * lat_rows
    f32 = jnp.float32
    bf16 = jnp.bfloat16
    parts, columns = filter_parts(lon_count)
    places = table_places(parts)

    def distance(lat):
        return jnp.minimum(lat, lat_count - 1 - lat)

    def is_polar(lat):
        return jnp.logical_and(distance(lat) >= 0, 15 * distance(lat) < 2 * (lat_count - 1))

    edge_ref[0] = low_ref[0].astype(f32)
    edge_ref[1] = high_ref[0].astype(f32)
    u_out[...] = u_ref[...]
    v_out[...] = v_ref[...]

    needs_filter = is_polar(first_lat)
    for offset in (-1, lat_rows - 1, lat_rows):
        needs_filter = jnp.logical_or(needs_filter, is_polar(first_lat + offset))

    @pl.when(needs_filter)
    def _():
        half, quarter, eighth = parts[0][2], parts[1][2], parts[2][2]
        half_wide, quarter_wide, eighth_wide = (padded_to(part[2]) for part in parts[:3])
        lats = [first_lat + j for j in range(lat_rows)]
        lats = lats + lats + [first_lat - 1, first_lat + lat_rows]
        for g in range(groups):
            if g < lat_rows:
                wind = u_ref[g].astype(f32)
            elif g < 2 * lat_rows:
                wind = v_ref[g - lat_rows].astype(f32)
            else:
                wind = edge_ref[g - 2 * lat_rows]
            real_ref[g, :, lon_count:] = jnp.zeros((level_rows, padded - lon_count), f32)
            real_ref[g, :, :lon_count] = wind
            near = real_ref[g, :, :half_wide]
            far = real_ref[g, :, half : half + half_wide]
            odd, even = near - far, near + far
            work_ref[g, :, :half_wide] = even
            near = even[:, :quarter_wide]
            far = work_ref[g, :, quarter : quarter + quarter_wide]
            two, even = near - far, near + far
            work_ref[g, :, half_wide : half_wide + quarter_wide] = even
            near = even[:, :eighth_wide]
            far = work_ref[g, :, half_wide + eighth : half_wide + eighth + eighth_wide]
            row = jnp.concatenate([odd, two, near - far, near + far], axis=1)
            high = row.astype(bf16).astype(f32)
            both = jnp.concatenate([high, row - high], axis=0)
            split_ref[2 * level_rows * g : 2 * level_rows * (g + 1), :] = both.astype(bf16)
        for (_, _, _, column), (top, left, size) in zip(parts, places):
            prod_ref[:, column : column + size] = jnp.dot(
                split_ref[:, column : column + size],
                table_ref[top : top + size, left : left + size],
                preferred_element_type=f32,
            )
        for g in range(0, groups, 2):
            pair = []
            for member in (g, g + 1):
                start = 2 * level_rows * member
                spectra = (
                    prod_ref[start : start + level_rows, :]
                    + prod_ref[start + level_rows : start + 2 * level_rows, :]
                )
                place = jnp.clip(distance(lats[member]), 0, distances - 1)
                pair.append(spectra * damp_ref[place])
            spec_ref[level_rows * g : level_rows * (g + 2), :] = jnp.concatenate(
                pair, axis=0
            ).astype(bf16)
        rows = groups * level_rows
        for (_, _, _, column), (top, left, size) in zip(parts, places):
            prod_ref[:rows, column : column + size] = lax.dot_general(
                spec_ref[:, column : column + size],
                table_ref[top : top + size, left : left + size],
                (((1,), (1,)), ((), ())),
                preferred_element_type=f32,
            )
        for g in range(groups):
            start = level_rows * g
            odd, two, four, eight = (
                prod_ref[start : start + level_rows, column : column + padded_to(points)]
                for _, _, points, column in parts
            )
            work_ref[g, :, :eighth_wide] = eight + four
            work_ref[g, :, eighth : 2 * eighth] = (eight - four)[:, :eighth]
            even = work_ref[g, :, :quarter_wide]
            work_ref[g, :, :quarter_wide] = even + two
            work_ref[g, :, quarter : 2 * quarter] = (even - two)[:, :quarter]
            even = work_ref[g, :, :half_wide]
            scale = 1.0 / lon_count
            real_ref[g, :, :half_wide] = (even + odd) * scale
            real_ref[g, :, half : 2 * half] = ((even - odd) * scale)[:, :half]
        for g in range(2 * lat_rows):
            out = u_out if g < lat_rows else v_out

            @pl.when(is_polar(lats[g]))
            def _():
                out[g % lat_rows] = real_ref[g, :, :lon_count].astype(bf16)

        for side in range(2):

            @pl.when(is_polar(lats[2 * lat_rows + side]))
            def _():
                smooth = real_ref[2 * lat_rows + side, :, :lon_count]
                edge_ref[side] = smooth.astype(bf16).astype(f32)

    whole = lon_count // LANES * LANES
    rest = lon_count - whole
    lane = lax.broadcasted_iota(jnp.int32, (level_rows, LANES), 1)

    def courant(wind):
        return jnp.clip(0.05 * wind, -0.15, 0.15)

    def extend(ref, index, value):
        ref[index, :, :lon_count] = value
        tail = jnp.where(
            lane < rest,
            ref[index, :, whole : whole + LANES],
            pltpu.roll(ref[index, :, :LANES], rest, 1),
        )
        ends = pltpu.roll(tail, LANES - rest, 1)
        return jnp.concatenate([ref[index, :, :whole], tail, ends], axis=1)

    def before(value):
        return pltpu.roll(value, 1, 1)

    def after(value):
        return pltpu.roll(value, padded - 1, 1)

    def plain(index, value):
        real_ref[index, :, :lon_count] = value
        return real_ref[index]

    fields_below = (low_ref[1].astype(f32), low_ref[2].astype(f32))
    courant_below = courant(edge_ref[0])
    flux_below = None
    for j in range(lat_rows):
        thick = thick_ref[j]
        mass = tracer_ref[j] * thick
        courant_here = courant(v_out[j].astype(f32))
        if j == 0:
            face = 0.5 * (courant_below + courant_here)
            face = jnp.where(first_lat == 0, jnp.zeros_like(face), face)
            flux_below = [
                jnp.maximum(face, 0.0) * below + jnp.minimum(face, 0.0) * here
                for below, here in zip(fields_below, (thick, mass))
            ]
        if j == lat_rows - 1:
            courant_above = courant(edge_ref[1])
            thick_above = high_ref[1].astype(f32)
            mass_above = high_ref[2].astype(f32)
        else:
            courant_above = courant(v_out[j + 1].astype(f32))
            thick_above = thick_ref[j + 1]
            mass_above = tracer_ref[j + 1] * thick_above
        face = 0.5 * (courant_here + courant_above)
        if j == lat_rows - 1:
            at_end = first_lat + lat_rows == lat_count
            face = jnp.where(at_end, jnp.zeros_like(face), face)
        rise, fall = jnp.maximum(face, 0.0), jnp.minimum(face, 0.0)
        flux_above = [rise * thick + fall * thick_above, rise * mass + fall * mass_above]
        courant_x = extend(real_ref, 0, courant(u_out[j].astype(f32)))
        face_x = 0.5 * (before(courant_x) + courant_x)
        rise_x, fall_x = jnp.maximum(face_x, 0.0), jnp.minimum(face_x, 0.0)
        moved = []
        for index, field in enumerate((thick, mass)):
            field_x = extend(real_ref, 1 + index, field)
            flux_x = rise_x * before(field_x) + fall_x * field_x
            across = flux_above[index] - flux_below[index]
            result = field_x - (after(flux_x) - flux_x) - plain(3 + index, across)
            moved.append(result)
        moved[0] = moved[0] - THICK_MID
        both = jnp.concatenate(moved, axis=0)
        for s in range(sectors):
            block = both[:, s * sector : s * sector + sector_wide]
            send_ref[s, 2 * level_rows * j : 2 * level_rows * (j + 1), :] = block.astype(bf16)
        flux_below = flux_above


def remap(index_ref, frac_ref, recv_ref, thick_out, tracer_out):
    lat_rows, level_count, sector = thick_out.shape
    sources, _, wide = recv_ref.shape
    level_rows = level_count // sources
    f32 = jnp.float32
    lanes = index_ref.shape[1]
    target = lax.broadcasted_iota(jnp.int32, (1, lanes), 1)
    own = index_ref[...] == target
    frac = frac_ref[...]
    inner = jnp.where(own, 1.0, frac)
    outer = jnp.where(own, frac, 0.0)
    inner_next = pltpu.roll(inner, lanes - 1, 1)
    outer_next = pltpu.roll(outer, lanes - 1, 1)
    rows = lax.broadcasted_iota(jnp.int32, (level_count, lanes), 0)
    columns = lax.broadcasted_iota(jnp.int32, (level_count, lanes), 1)
    diagonal = rows == columns

    def column(row):
        spread = jnp.where(diagonal, jnp.broadcast_to(row, diagonal.shape), 0.0)
        return jnp.broadcast_to(jnp.sum(spread, axis=1, keepdims=True), (level_count, wide))

    below, here, above = column(1.0 - inner), column(inner_next - outer), column(outer_next)
    place = lax.broadcasted_iota(jnp.int32, (level_rows, wide), 0)
    top, bottom = place == 0, place == level_rows - 1
    for j in range(lat_rows):
        blocks = [
            recv_ref[source, 2 * level_rows * j : 2 * level_rows * (j + 1), :].astype(f32)
            for source in range(sources)
        ]
        results = []
        for index in range(2):
            layers = [block[level_rows * index : level_rows * (index + 1)] for block in blocks]
            if index == 0:
                layers = [layer + THICK_MID for layer in layers]
            down = [pltpu.roll(layer, 1, 0) for layer in layers]
            up = [pltpu.roll(layer, level_rows - 1, 0) for layer in layers]
            outs = []
            for source in range(sources):
                chosen = slice(level_rows * source, level_rows * (source + 1))
                lower = jnp.where(top, down[max(source - 1, 0)], down[source])
                higher = jnp.where(bottom, up[min(source + 1, sources - 1)], up[source])
                outs.append(
                    below[chosen] * lower + here[chosen] * layers[source] + above[chosen] * higher
                )
            results.append(outs)
        for source in range(sources):
            chosen = slice(level_rows * source, level_rows * (source + 1))
            thick, mass = results[0][source], results[1][source]
            thick_out[j, chosen, :] = thick[:, :sector]
            tracer_out[j, chosen, :] = (mass / thick)[:, :sector]


def per_device(u_wind, v_wind, thickness, tracer, remap_index, remap_frac):
    lat_rows, level_rows, lon_count = u_wind.shape
    lat_devices = lax.axis_size("lat")
    lat_count = lat_rows * lat_devices
    sectors = lax.axis_size("lev")
    level_count = level_rows * sectors
    sector = lon_count // sectors
    sector_wide = padded_to(sector)
    tables, damping = filter_tables(lat_count, lon_count)
    columns = damping.shape[2]
    padded = (lon_count // LANES + 2) * LANES
    f32, bf16 = jnp.float32, jnp.bfloat16

    def edge(row):
        thick = thickness[row]
        mass = tracer[row] * thick
        return jnp.stack([v_wind[row], thick.astype(bf16), mass.astype(bf16)])

    forward = [(i, i + 1) for i in range(lat_devices - 1)]
    backward = [(target, source) for source, target in forward]
    low = lax.ppermute(edge(lat_rows - 1), "lat", forward)
    high = lax.ppermute(edge(0), "lat", backward)
    groups = 2 * lat_rows + 2
    u_filtered, v_filtered, send = pl.pallas_call(
        functools.partial(filter_advect, lat_count),
        out_shape=(
            jax.ShapeDtypeStruct(u_wind.shape, bf16),
            jax.ShapeDtypeStruct(v_wind.shape, bf16),
            jax.ShapeDtypeStruct((sectors, 2 * lat_rows * level_rows, sector_wide), bf16),
        ),
        scratch_shapes=[
            pltpu.VMEM((groups, level_rows, padded), f32),
            pltpu.VMEM((groups, level_rows, padded), f32),
            pltpu.VMEM((2 * groups * level_rows, columns), bf16),
            pltpu.VMEM((2 * groups * level_rows, columns), f32),
            pltpu.VMEM((groups * level_rows, columns), bf16),
            pltpu.VMEM((2, level_rows, lon_count), f32),
        ],
        compiler_params=pltpu.CompilerParams(vmem_limit_bytes=40 * 1024 * 1024),
        name="filter_advect",
    )(u_wind, v_wind, thickness, tracer, low, high, tables, damping)
    recv = lax.all_to_all(send, "lev", split_axis=0, concat_axis=0, tiled=True)
    spare = -(level_count + 1) % LANES
    index_row = jnp.pad(remap_index, (0, spare))[None, :]
    frac_row = jnp.pad(remap_frac, (0, spare))[None, :]
    out = jax.ShapeDtypeStruct((lat_rows, level_count, sector), f32)
    thick_out, tracer_out = pl.pallas_call(
        remap,
        out_shape=(out, out),
        compiler_params=pltpu.CompilerParams(vmem_limit_bytes=32 * 1024 * 1024),
        name="remap",
    )(index_row, frac_row, recv)
    return u_filtered, v_filtered, thick_out, tracer_out


def solution(mesh):
    placed = (
        P("lat", "lev", None),
        P("lat", "lev", None),
        P("lat", "lev", None),
        P("lat", "lev", None),
        P(),
        P(),
    )
    return jax.shard_map(
        per_device,
        mesh=mesh,
        in_specs=placed,
        out_specs=(
            P("lat", "lev", None),
            P("lat", "lev", None),
            P("lat", None, "lev"),
            P("lat", None, "lev"),
        ),
        check_vma=False,
    )
```

```python
import functools
import math

import jax
import jax.numpy as jnp
import ml_dtypes
import numpy as np
from jax import lax
from jax.experimental import pallas as pl
from jax.experimental.pallas import tpu as pltpu
from jax.sharding import PartitionSpec as P

COS_EDGE = math.cos(66.0 * math.pi / 180.0)
LANES = 128
THICK_MID = 1.25


def padded_to(count):
    return -(-count // LANES) * LANES


def filter_parts(lon_count):
    parts = []
    column = 0
    for first, step, points in (
        (1, 2, lon_count // 2),
        (2, 4, lon_count // 4),
        (4, 8, lon_count // 8),
        (0, 8, lon_count // 8),
    ):
        parts.append((first, step, points, column))
        column += padded_to(points)
    return parts, column


def table_places(parts):
    odd, two, four, eight = (padded_to(part[2]) for part in parts)
    return [(0, 0, odd), (0, odd, two), (two, odd, four), (two, odd + four, eight)]


def filter_tables(lat_count, lon_count):
    phase = 2.0 * np.pi * np.arange(lon_count) / lon_count
    rounded = (np.cos(phase) + np.sin(phase)).astype(np.float32).astype(ml_dtypes.bfloat16)
    polar = [d for d in range((lat_count + 1) // 2) if 15 * d < 2 * (lat_count - 1)]
    ratio = (np.sin(np.pi * np.array(polar, np.float64) / (lat_count - 1)) / COS_EDGE) ** 2
    wave = np.arange(lon_count)
    wave = np.minimum(wave, lon_count - wave)
    sine_square = np.sin(np.pi * wave / lon_count) ** 2
    sine_square[0] = 1.0
    values = np.minimum(1.0, ratio[:, None] / sine_square[None, :])
    values[:, 0] = 1.0

    parts, columns = filter_parts(lon_count)
    places = table_places(parts)
    tables = np.zeros((places[0][2], places[0][2] + places[1][2]), ml_dtypes.bfloat16)
    damping = np.zeros((len(polar), 1, columns), np.float32)
    for (first, step, points, column), (row, left, _) in zip(parts, places):
        waves = first + step * np.arange(points)
        tables[row : row + points, left : left + points] = rounded[
            np.arange(points)[:, None] * waves[None, :] % lon_count
        ]
        damping[:, 0, column : column + points] = values[:, waves]
    return tables, damping


def distance(lat, lat_count):
    return jnp.minimum(lat, lat_count - 1 - lat)


def is_polar(lat, lat_count):
    d = distance(lat, lat_count)
    return jnp.logical_and(d >= 0, 15 * d < 2 * (lat_count - 1))


def band_is_polar(first_lat, lat_rows, lat_count):
    found = is_polar(first_lat, lat_count)
    for offset in (-1, lat_rows - 1, lat_rows):
        found = jnp.logical_or(found, is_polar(first_lat + offset, lat_count))
    return found


def pack(v_hbm, thick_hbm, tracer_hbm, near_out, next_out, v_buf, thick_buf, tracer_buf, sems):
    lat_rows = v_hbm.shape[0]
    copies = []
    for side, row in enumerate((0, lat_rows - 1)):
        for source, target in ((v_hbm, v_buf), (thick_hbm, thick_buf), (tracer_hbm, tracer_buf)):
            copy = pltpu.make_async_copy(source.at[row], target.at[side], sems.at[len(copies)])
            copy.start()
            copies.append(copy)
    for copy in copies:
        copy.wait()
    odd = lax.axis_index("lat") % 2
    for out, side in ((near_out, 1 - odd), (next_out, odd)):
        thick = thick_buf[side]
        out[0] = v_buf[side]
        out[1] = thick.astype(jnp.bfloat16)
        out[2] = (tracer_buf[side] * thick).astype(jnp.bfloat16)


def load(lat_count, *refs):
    sems = refs[-1]
    half = len(refs) // 2
    sources, targets = refs[:half], refs[half:-1]
    always = len(sources) - 2
    lat_rows = sources[0].shape[0]
    copies = [
        pltpu.make_async_copy(source, target, sems.at[place])
        for place, (source, target) in enumerate(zip(sources, targets))
    ]
    polar = band_is_polar(lax.axis_index("lat") * lat_rows, lat_rows, lat_count)

    @pl.when(polar)
    def _():
        for copy in copies[always:]:
            copy.start()

    for copy in copies[:always]:
        copy.start()
    for copy in copies[:always]:
        copy.wait()

    @pl.when(polar)
    def _():
        for copy in copies[always:]:
            copy.wait()


def filter_advect(
    lat_count,
    u_ref,
    v_ref,
    thick_ref,
    tracer_ref,
    table_ref,
    damp_ref,
    near_ref,
    next_ref,
    u_hbm,
    v_hbm,
    send_ref,
    u_out,
    v_out,
    real_ref,
    work_ref,
    split_ref,
    prod_ref,
    spec_ref,
    edge_ref,
    sems,
):
    lat_rows, level_rows, lon_count = u_ref.shape
    sectors = send_ref.shape[0]
    sector_wide = send_ref.shape[2]
    sector = lon_count // sectors
    groups, _, padded = real_ref.shape
    distances = damp_ref.shape[0]
    first_lat = lax.axis_index("lat") * lat_rows
    f32 = jnp.float32
    bf16 = jnp.bfloat16
    parts, columns = filter_parts(lon_count)
    places = table_places(parts)

    odd_device = lax.axis_index("lat") % 2
    for side in range(2):
        for source, odd in ((near_ref, 1 - side), (next_ref, side)):

            @pl.when(odd_device == odd)
            def _():
                edge_ref[side] = source[...].astype(f32)

    u_out[...] = u_ref[...]
    v_out[...] = v_ref[...]

    @pl.when(band_is_polar(first_lat, lat_rows, lat_count))
    def _():
        half, quarter, eighth = parts[0][2], parts[1][2], parts[2][2]
        half_wide, quarter_wide, eighth_wide = (padded_to(part[2]) for part in parts[:3])
        lats = [first_lat + j for j in range(lat_rows)]
        lats = lats + lats + [first_lat - 1, first_lat + lat_rows]
        for g in range(groups):
            if g < lat_rows:
                wind = u_ref[g].astype(f32)
            elif g < 2 * lat_rows:
                wind = v_ref[g - lat_rows].astype(f32)
            else:
                wind = edge_ref[g - 2 * lat_rows, 0]
            real_ref[g, :, lon_count:] = jnp.zeros((level_rows, padded - lon_count), f32)
            real_ref[g, :, :lon_count] = wind
            near = real_ref[g, :, :half_wide]
            far = real_ref[g, :, half : half + half_wide]
            odd, even = near - far, near + far
            work_ref[g, :, :half_wide] = even
            near = even[:, :quarter_wide]
            far = work_ref[g, :, quarter : quarter + quarter_wide]
            two, even = near - far, near + far
            work_ref[g, :, half_wide : half_wide + quarter_wide] = even
            near = even[:, :eighth_wide]
            far = work_ref[g, :, half_wide + eighth : half_wide + eighth + eighth_wide]
            row = jnp.concatenate([odd, two, near - far, near + far], axis=1)
            high = row.astype(bf16).astype(f32)
            both = jnp.concatenate([high, row - high], axis=0)
            split_ref[2 * level_rows * g : 2 * level_rows * (g + 1), :] = both.astype(bf16)
        for (_, _, _, column), (top, left, size) in zip(parts, places):
            prod_ref[:, column : column + size] = jnp.dot(
                split_ref[:, column : column + size],
                table_ref[top : top + size, left : left + size],
                preferred_element_type=f32,
            )
        for g in range(0, groups, 2):
            pair = []
            for member in (g, g + 1):
                start = 2 * level_rows * member
                spectra = (
                    prod_ref[start : start + level_rows, :]
                    + prod_ref[start + level_rows : start + 2 * level_rows, :]
                )
                place = jnp.clip(distance(lats[member], lat_count), 0, distances - 1)
                pair.append(spectra * damp_ref[place])
            spec_ref[level_rows * g : level_rows * (g + 2), :] = jnp.concatenate(
                pair, axis=0
            ).astype(bf16)
        rows = groups * level_rows
        for (_, _, _, column), (top, left, size) in zip(parts, places):
            prod_ref[:rows, column : column + size] = lax.dot_general(
                spec_ref[:, column : column + size],
                table_ref[top : top + size, left : left + size],
                (((1,), (1,)), ((), ())),
                preferred_element_type=f32,
            )
        for g in range(groups):
            start = level_rows * g
            odd, two, four, eight = (
                prod_ref[start : start + level_rows, column : column + padded_to(points)]
                for _, _, points, column in parts
            )
            work_ref[g, :, :eighth_wide] = eight + four
            work_ref[g, :, eighth : 2 * eighth] = (eight - four)[:, :eighth]
            even = work_ref[g, :, :quarter_wide]
            work_ref[g, :, :quarter_wide] = even + two
            work_ref[g, :, quarter : 2 * quarter] = (even - two)[:, :quarter]
            even = work_ref[g, :, :half_wide]
            scale = 1.0 / lon_count
            real_ref[g, :, :half_wide] = (even + odd) * scale
            real_ref[g, :, half : 2 * half] = ((even - odd) * scale)[:, :half]
        for g in range(2 * lat_rows):
            out = u_out if g < lat_rows else v_out

            @pl.when(is_polar(lats[g], lat_count))
            def _():
                out[g % lat_rows] = real_ref[g, :, :lon_count].astype(bf16)

        for side in range(2):

            @pl.when(is_polar(lats[2 * lat_rows + side], lat_count))
            def _():
                smooth = real_ref[2 * lat_rows + side, :, :lon_count]
                edge_ref[side, 0] = smooth.astype(bf16).astype(f32)

    winds_out = [
        pltpu.make_async_copy(u_out, u_hbm, sems.at[0]),
        pltpu.make_async_copy(v_out, v_hbm, sems.at[1]),
    ]
    for copy in winds_out:
        copy.start()

    whole = lon_count // LANES * LANES
    rest = lon_count - whole
    lane = lax.broadcasted_iota(jnp.int32, (level_rows, LANES), 1)

    def courant(wind):
        return jnp.clip(0.05 * wind, -0.15, 0.15)

    def extend(ref, index, value):
        ref[index, :, :lon_count] = value
        tail = jnp.where(
            lane < rest,
            ref[index, :, whole : whole + LANES],
            pltpu.roll(ref[index, :, :LANES], rest, 1),
        )
        ends = pltpu.roll(tail, LANES - rest, 1)
        return jnp.concatenate([ref[index, :, :whole], tail, ends], axis=1)

    def before(value):
        return pltpu.roll(value, 1, 1)

    def after(value):
        return pltpu.roll(value, padded - 1, 1)

    def plain(index, value):
        real_ref[index, :, :lon_count] = value
        return real_ref[index]

    fields_below = (edge_ref[0, 1], edge_ref[0, 2])
    courant_below = courant(edge_ref[0, 0])
    flux_below = None
    for j in range(lat_rows):
        thick = thick_ref[j]
        mass = tracer_ref[j] * thick
        courant_here = courant(v_out[j].astype(f32))
        if j == 0:
            face = 0.5 * (courant_below + courant_here)
            face = jnp.where(first_lat == 0, jnp.zeros_like(face), face)
            flux_below = [
                jnp.maximum(face, 0.0) * below + jnp.minimum(face, 0.0) * here
                for below, here in zip(fields_below, (thick, mass))
            ]
        if j == lat_rows - 1:
            courant_above = courant(edge_ref[1, 0])
            thick_above, mass_above = edge_ref[1, 1], edge_ref[1, 2]
        else:
            courant_above = courant(v_out[j + 1].astype(f32))
            thick_above = thick_ref[j + 1]
            mass_above = tracer_ref[j + 1] * thick_above
        face = 0.5 * (courant_here + courant_above)
        if j == lat_rows - 1:
            at_end = first_lat + lat_rows == lat_count
            face = jnp.where(at_end, jnp.zeros_like(face), face)
        rise, fall = jnp.maximum(face, 0.0), jnp.minimum(face, 0.0)
        flux_above = [rise * thick + fall * thick_above, rise * mass + fall * mass_above]
        courant_x = extend(real_ref, 0, courant(u_out[j].astype(f32)))
        face_x = 0.5 * (before(courant_x) + courant_x)
        rise_x, fall_x = jnp.maximum(face_x, 0.0), jnp.minimum(face_x, 0.0)
        moved = []
        for index, field in enumerate((thick, mass)):
            field_x = extend(real_ref, 1 + index, field)
            flux_x = rise_x * before(field_x) + fall_x * field_x
            across = flux_above[index] - flux_below[index]
            result = field_x - (after(flux_x) - flux_x) - plain(3 + index, across)
            moved.append(result)
        moved[0] = moved[0] - THICK_MID
        both = jnp.concatenate(moved, axis=0)
        for s in range(sectors):
            block = both[:, s * sector : s * sector + sector_wide]
            send_ref[s, 2 * level_rows * j : 2 * level_rows * (j + 1), :] = block.astype(bf16)
        flux_below = flux_above
    for copy in winds_out:
        copy.wait()


def remap(
    index_ref, frac_ref, recv_ref, thick_hbm, tracer_hbm, thick_out, tracer_out, sems
):
    lat_rows, level_count, sector = thick_out.shape
    sources, _, wide = recv_ref.shape
    level_rows = level_count // sources
    f32 = jnp.float32
    lanes = index_ref.shape[1]
    target = lax.broadcasted_iota(jnp.int32, (1, lanes), 1)
    own = index_ref[...] == target
    frac = frac_ref[...]
    inner = jnp.where(own, 1.0, frac)
    outer = jnp.where(own, frac, 0.0)
    inner_next = pltpu.roll(inner, lanes - 1, 1)
    outer_next = pltpu.roll(outer, lanes - 1, 1)
    rows = lax.broadcasted_iota(jnp.int32, (level_count, lanes), 0)
    columns = lax.broadcasted_iota(jnp.int32, (level_count, lanes), 1)
    diagonal = rows == columns

    def column(row):
        spread = jnp.where(diagonal, jnp.broadcast_to(row, diagonal.shape), 0.0)
        return jnp.broadcast_to(jnp.sum(spread, axis=1, keepdims=True), (level_count, wide))

    below, here, above = column(1.0 - inner), column(inner_next - outer), column(outer_next)
    place = lax.broadcasted_iota(jnp.int32, (level_rows, wide), 0)
    top, bottom = place == 0, place == level_rows - 1
    copies = []
    for j in range(lat_rows):
        blocks = [
            recv_ref[source, 2 * level_rows * j : 2 * level_rows * (j + 1), :].astype(f32)
            for source in range(sources)
        ]
        results = []
        for index in range(2):
            layers = [block[level_rows * index : level_rows * (index + 1)] for block in blocks]
            if index == 0:
                layers = [layer + THICK_MID for layer in layers]
            down = [pltpu.roll(layer, 1, 0) for layer in layers]
            up = [pltpu.roll(layer, level_rows - 1, 0) for layer in layers]
            outs = []
            for source in range(sources):
                chosen = slice(level_rows * source, level_rows * (source + 1))
                lower = jnp.where(top, down[max(source - 1, 0)], down[source])
                higher = jnp.where(bottom, up[min(source + 1, sources - 1)], up[source])
                outs.append(
                    below[chosen] * lower + here[chosen] * layers[source] + above[chosen] * higher
                )
            results.append(outs)
        for source in range(sources):
            chosen = slice(level_rows * source, level_rows * (source + 1))
            thick, mass = results[0][source], results[1][source]
            thick_out[j, chosen, :] = thick[:, :sector]
            tracer_out[j, chosen, :] = (mass / thick)[:, :sector]
        for source, target in ((thick_out, thick_hbm), (tracer_out, tracer_hbm)):
            copy = pltpu.make_async_copy(source.at[j], target.at[j], sems.at[len(copies)])
            copy.start()
            copies.append(copy)
    for copy in copies:
        copy.wait()


def per_device(u_wind, v_wind, thickness, tracer, remap_index, remap_frac):
    lat_rows, level_rows, lon_count = u_wind.shape
    lat_devices = lax.axis_size("lat")
    lat_count = lat_rows * lat_devices
    sectors = lax.axis_size("lev")
    level_count = level_rows * sectors
    sector = lon_count // sectors
    sector_wide = padded_to(sector)
    tables, damping = filter_tables(lat_count, lon_count)
    columns = damping.shape[2]
    padded = (lon_count // LANES + 2) * LANES
    f32, bf16 = jnp.float32, jnp.bfloat16

    in_hbm = pl.BlockSpec(memory_space=pltpu.HBM)
    in_vmem = pl.BlockSpec(memory_space=pltpu.VMEM)
    limit = pltpu.CompilerParams(vmem_limit_bytes=40 * 1024 * 1024)
    edges = (3, level_rows, lon_count)

    def stay(array):
        return pltpu.with_memory_space_constraint(jnp.asarray(array), pltpu.HBM)

    near, beyond = pl.pallas_call(
        pack,
        out_shape=(pltpu.VMEM(edges, bf16), pltpu.VMEM(edges, bf16)),
        in_specs=[in_hbm] * 3,
        out_specs=(in_vmem, in_vmem),
        scratch_shapes=[
            pltpu.VMEM((2, level_rows, lon_count), bf16),
            pltpu.VMEM((2, level_rows, lon_count), f32),
            pltpu.VMEM((2, level_rows, lon_count), f32),
            pltpu.SemaphoreType.DMA((6,)),
        ],
        compiler_params=limit,
        name="pack",
    )(*(stay(array) for array in (v_wind, thickness, tracer)))
    swap_near = [(i, i ^ 1) for i in range(lat_devices)]
    swap_next = [(i, i - 1 + 2 * (i % 2)) for i in range(1, lat_devices - 1)]
    beyond = lax.ppermute(beyond, "lat", swap_next)
    near = lax.ppermute(near, "lat", swap_near)

    arrays = (u_wind, v_wind, thickness, tracer, tables, damping)
    moved_bytes = sum(array.size * array.dtype.itemsize for array in arrays)
    loaded = pl.pallas_call(
        functools.partial(load, lat_count),
        out_shape=[pltpu.VMEM(array.shape, array.dtype) for array in arrays],
        in_specs=[in_hbm] * len(arrays),
        out_specs=[in_vmem] * len(arrays),
        scratch_shapes=[pltpu.SemaphoreType.DMA((len(arrays),))],
        compiler_params=limit,
        cost_estimate=pl.CostEstimate(flops=0, bytes_accessed=moved_bytes, transcendentals=0),
        name="load",
    )(*(stay(array) for array in arrays))
    groups = 2 * lat_rows + 2
    u_filtered, v_filtered, send = pl.pallas_call(
        functools.partial(filter_advect, lat_count),
        out_shape=(
            pltpu.HBM(u_wind.shape, bf16),
            pltpu.HBM(v_wind.shape, bf16),
            pltpu.VMEM((sectors, 2 * lat_rows * level_rows, sector_wide), bf16),
        ),
        in_specs=[in_vmem] * (len(arrays) + 2),
        out_specs=(in_hbm, in_hbm, in_vmem),
        scratch_shapes=[
            pltpu.VMEM(u_wind.shape, bf16),
            pltpu.VMEM(v_wind.shape, bf16),
            pltpu.VMEM((groups, level_rows, padded), f32),
            pltpu.VMEM((groups, level_rows, padded), f32),
            pltpu.VMEM((2 * groups * level_rows, columns), bf16),
            pltpu.VMEM((2 * groups * level_rows, columns), f32),
            pltpu.VMEM((groups * level_rows, columns), bf16),
            pltpu.VMEM((2, 3, level_rows, lon_count), f32),
            pltpu.SemaphoreType.DMA((2,)),
        ],
        compiler_params=limit,
        name="filter_advect",
    )(*loaded, near, beyond)
    recv = lax.all_to_all(send, "lev", split_axis=0, concat_axis=0, tiled=True)
    spare = -(level_count + 1) % LANES
    index_row = jnp.pad(remap_index, (0, spare))[None, :]
    frac_row = jnp.pad(remap_frac, (0, spare))[None, :]
    shape = (lat_rows, level_count, sector)
    thick_out, tracer_out = pl.pallas_call(
        remap,
        out_shape=(pltpu.HBM(shape, f32), pltpu.HBM(shape, f32)),
        in_specs=[in_vmem] * 3,
        out_specs=(in_hbm, in_hbm),
        scratch_shapes=[
            pltpu.VMEM(shape, f32),
            pltpu.VMEM(shape, f32),
            pltpu.SemaphoreType.DMA((2 * lat_rows,)),
        ],
        compiler_params=limit,
        name="remap",
    )(index_row, frac_row, recv)
    return u_filtered, v_filtered, thick_out, tracer_out


def solution(mesh):
    placed = (
        P("lat", "lev", None),
        P("lat", "lev", None),
        P("lat", "lev", None),
        P("lat", "lev", None),
        P(),
        P(),
    )
    return jax.shard_map(
        per_device,
        mesh=mesh,
        in_specs=placed,
        out_specs=(
            P("lat", "lev", None),
            P("lat", "lev", None),
            P("lat", None, "lev"),
            P("lat", None, "lev"),
        ),
        check_vma=False,
    )
```

```python
import functools
import math

import jax
import jax.numpy as jnp
import ml_dtypes
import numpy as np
from jax import lax
from jax.experimental import pallas as pl
from jax.experimental.pallas import tpu as pltpu
from jax.sharding import PartitionSpec as P

COS_EDGE = math.cos(66.0 * math.pi / 180.0)
LANES = 128
THICK_MID = 1.25


def padded_to(count):
    return -(-count // LANES) * LANES


def filter_parts(lon_count):
    parts = []
    column = 0
    for first, step, points in (
        (1, 2, lon_count // 2),
        (2, 4, lon_count // 4),
        (4, 8, lon_count // 8),
        (0, 8, lon_count // 8),
    ):
        parts.append((first, step, points, column))
        column += padded_to(points)
    return parts, column


def table_places(parts):
    odd, two, four, eight = (padded_to(part[2]) for part in parts)
    return [(0, 0, odd), (0, odd, two), (two, odd, four), (two, odd + four, eight)]


def filter_tables(lat_count, lon_count):
    phase = 2.0 * np.pi * np.arange(lon_count) / lon_count
    rounded = (np.cos(phase) + np.sin(phase)).astype(np.float32).astype(ml_dtypes.bfloat16)
    polar = [d for d in range((lat_count + 1) // 2) if 15 * d < 2 * (lat_count - 1)]
    ratio = (np.sin(np.pi * np.array(polar, np.float64) / (lat_count - 1)) / COS_EDGE) ** 2
    wave = np.arange(lon_count)
    wave = np.minimum(wave, lon_count - wave)
    sine_square = np.sin(np.pi * wave / lon_count) ** 2
    sine_square[0] = 1.0
    values = np.minimum(1.0, ratio[:, None] / sine_square[None, :])
    values[:, 0] = 1.0

    parts, columns = filter_parts(lon_count)
    places = table_places(parts)
    tables = np.zeros((places[0][2], places[0][2] + places[1][2]), ml_dtypes.bfloat16)
    damping = np.zeros((len(polar), 1, columns), np.float32)
    for (first, step, points, column), (row, left, _) in zip(parts, places):
        waves = first + step * np.arange(points)
        values_here = rounded[np.arange(points)[:, None] * waves[None, :] % lon_count]
        tables[row : row + points, left : left + points] = values_here
        damping[:, 0, column : column + points] = values[:, waves]
    return tables, damping


def distance(lat, lat_count):
    return jnp.minimum(lat, lat_count - 1 - lat)


def is_polar(lat, lat_count):
    d = distance(lat, lat_count)
    return jnp.logical_and(d >= 0, 15 * d < 2 * (lat_count - 1))


def band_is_polar(first_lat, lat_rows, lat_count):
    found = is_polar(first_lat, lat_count)
    for offset in (-1, lat_rows - 1, lat_rows):
        found = jnp.logical_or(found, is_polar(first_lat + offset, lat_count))
    return found


def pack(v_hbm, thick_hbm, tracer_hbm, near_out, next_out, v_buf, thick_buf, tracer_buf, sems):
    lat_rows = v_hbm.shape[0]
    copies = []
    for side, row in enumerate((0, lat_rows - 1)):
        for source, target in ((v_hbm, v_buf), (thick_hbm, thick_buf), (tracer_hbm, tracer_buf)):
            copy = pltpu.make_async_copy(source.at[row], target.at[side], sems.at[len(copies)])
            copy.start()
            copies.append(copy)
    for copy in copies:
        copy.wait()
    odd = lax.axis_index("lat") % 2
    for out, side in ((near_out, 1 - odd), (next_out, odd)):
        thick = thick_buf[side]
        out[0] = v_buf[side]
        out[1] = thick.astype(jnp.bfloat16)
        out[2] = (tracer_buf[side] * thick).astype(jnp.bfloat16)


def courant(wind):
    return jnp.clip(0.05 * wind, -0.15, 0.15)


def loop(count, body):
    def step(place, carry):
        body(place)
        return carry

    lax.fori_loop(0, count, step, 0)


def rows_at(place, count):
    return pl.ds(pl.multiple_of(place * count, count), count)


def up_and_down(face):
    return jnp.maximum(face, 0.0), jnp.minimum(face, 0.0)


def to_sectors(send_ref, moved_ref, j, sector):
    sectors, _, sector_wide = send_ref.shape
    height = moved_ref.shape[1]
    for s in range(sectors):
        block = moved_ref[j, :, s * sector : s * sector + sector_wide]
        send_ref[s, rows_at(j, height), :] = block.astype(send_ref.dtype)


def transport(j, wind_ref, row_ref, real_ref, moved_ref, least_face, most_face):
    level_rows, lon_count = row_ref.shape[2:]
    padded = real_ref.shape[2]
    whole = lon_count // LANES * LANES
    rest = lon_count - whole
    lane = lax.broadcasted_iota(jnp.int32, (level_rows, LANES), 1)

    def extend(index, value):
        real_ref[index, :, :lon_count] = value
        tail = jnp.where(
            lane < rest,
            real_ref[index, :, whole : whole + LANES],
            pltpu.roll(real_ref[index, :, :LANES], rest, 1),
        )
        ends = pltpu.roll(tail, LANES - rest, 1)
        real_ref[index, :, whole : whole + LANES] = tail
        real_ref[index, :, whole + LANES :] = ends
        return real_ref[index]

    def before(value):
        return pltpu.roll(value, 1, 1)

    def after(value):
        return pltpu.roll(value, padded - 1, 1)

    def face_y(f):
        face = 0.5 * (courant(row_ref[0, f]) + courant(row_ref[0, f + 1]))
        inside = jnp.logical_and(f >= least_face, f <= most_face)
        return up_and_down(face * jnp.where(inside, 1.0, 0.0))

    (rise_below, fall_below), (rise_above, fall_above) = face_y(j), face_y(j + 1)
    courant_x = extend(0, courant(wind_ref[j].astype(jnp.float32)))
    rise_x, fall_x = up_and_down(0.5 * (before(courant_x) + courant_x))
    for i in range(2):
        below, here, above = (row_ref[1 + i, j + k] for k in range(3))
        field = extend(1 + i, here)
        flux_x = rise_x * before(field) + fall_x * field
        across = rise_above * here + fall_above * above - rise_below * below - fall_below * here
        result = field - (after(flux_x) - flux_x)
        if i == 0:
            result = result - THICK_MID
        moved_ref[j, i * level_rows : (i + 1) * level_rows, :lon_count] = (
            result[:, :lon_count] - across
        )


def band_weights(index_ref, frac_ref, weight_ref):
    _, level_count, wide = weight_ref.shape

    def inner(k):
        return jnp.where(index_ref[k] == k, 1.0, frac_ref[k])

    def outer(k):
        return jnp.where(index_ref[k] == k, frac_ref[k], 0.0)

    def weigh(k):
        for place, weight in enumerate(
            (1.0 - inner(k), inner(k + 1) - outer(k), outer(k + 1))
        ):
            weight_ref[place, pl.ds(k, 1), :] = jnp.full((1, wide), weight, jnp.float32)

    loop(level_count, weigh)


def load(
    lat_count,
    index_hbm,
    frac_hbm,
    u_hbm,
    v_hbm,
    thick_hbm,
    tracer_hbm,
    table_hbm,
    damp_hbm,
    u_ref,
    v_ref,
    thick_ref,
    tracer_ref,
    table_ref,
    damp_ref,
    u_out,
    v_out,
    send_ref,
    moved_ref,
    weight_ref,
    row_ref,
    real_ref,
    index_ref,
    frac_ref,
    sems,
    table_sems,
):
    lat_rows, level_rows, lon_count = u_ref.shape
    f32 = jnp.float32
    polar = band_is_polar(lax.axis_index("lat") * lat_rows, lat_rows, lat_count)
    inputs = [
        pltpu.make_async_copy(source, target, sems.at[place])
        for place, (source, target) in enumerate(
            ((v_hbm, v_ref), (thick_hbm, thick_ref), (tracer_hbm, tracer_ref), (u_hbm, u_ref))
        )
    ]
    tables = [pltpu.make_async_copy(damp_hbm, damp_ref, sems.at[4])]
    chunks = table_sems.shape[0]
    height = table_hbm.shape[0] // chunks
    for chunk in range(chunks):
        part = pl.ds(chunk * height, height)
        tables.append(
            pltpu.make_async_copy(table_hbm.at[part], table_ref.at[part], table_sems.at[chunk])
        )
    for copy in inputs:
        copy.start()

    @pl.when(polar)
    def _():
        for copy in tables:
            copy.start()

    scalars = [
        pltpu.make_async_copy(index_hbm, index_ref, sems.at[7]),
        pltpu.make_async_copy(frac_hbm, frac_ref, sems.at[8]),
    ]
    for copy in scalars:
        copy.start()

    def weigh():
        for copy in scalars:
            copy.wait()
        band_weights(index_ref, frac_ref, weight_ref)

    @pl.when(polar)
    def _():
        weigh()
        for copy in inputs:
            copy.wait()
        for copy in tables:
            copy.wait()

    @pl.when(jnp.logical_not(polar))
    def _():
        for copy in inputs:
            copy.wait()
        winds = [
            pltpu.make_async_copy(u_ref, u_out, sems.at[5]),
            pltpu.make_async_copy(v_ref, v_out, sems.at[6]),
        ]
        for copy in winds:
            copy.start()
        blank = jnp.zeros((level_rows, lon_count), f32)
        for place in range(3):
            row_ref[place, 0] = blank
            row_ref[place, lat_rows + 1] = blank

        def prepare(j):
            thick = thick_ref[j]
            row_ref[0, j + 1] = v_ref[j].astype(f32)
            row_ref[1, j + 1] = thick
            row_ref[2, j + 1] = tracer_ref[j] * thick

        loop(lat_rows, prepare)

        def advect(j):
            transport(j, u_ref, row_ref, real_ref, moved_ref, 1, lat_rows - 1)

            @pl.when(jnp.logical_and(j > 0, j < lat_rows - 1))
            def _():
                to_sectors(send_ref, moved_ref, j, lon_count // send_ref.shape[0])

        loop(lat_rows, advect)
        weigh()
        for copy in winds:
            copy.wait()


def filter_advect(
    lat_count,
    u_ref,
    v_ref,
    thick_ref,
    tracer_ref,
    table_ref,
    damp_ref,
    partial_ref,
    near_ref,
    next_ref,
    u_held,
    v_held,
    send_held,
    u_hbm,
    v_hbm,
    send_ref,
    u_out,
    v_out,
    real_ref,
    work_ref,
    split_ref,
    prod_ref,
    spec_ref,
    row_ref,
    moved_ref,
    sems,
):
    lat_rows, level_rows, lon_count = u_ref.shape
    groups, _, padded = real_ref.shape
    distances = damp_ref.shape[0]
    first_lat = lax.axis_index("lat") * lat_rows
    f32 = jnp.float32
    bf16 = jnp.bfloat16
    parts, columns = filter_parts(lon_count)
    places = table_places(parts)
    odd_device = lax.axis_index("lat") % 2
    polar = band_is_polar(first_lat, lat_rows, lat_count)

    for side in range(2):
        for source, odd in ((near_ref, 1 - side), (next_ref, side)):

            @pl.when(odd_device == odd)
            def _():
                for place in range(3):
                    row_ref[place, side * (lat_rows + 1)] = source[place].astype(f32)

    @pl.when(jnp.logical_not(polar))
    def _():
        for side, j in enumerate((0, lat_rows - 1)):
            outer = side * (lat_rows + 1)
            own = courant(v_ref[j].astype(f32))
            face = 0.5 * (courant(row_ref[0, outer]) + own)
            at_pole = first_lat + side * lat_rows == side * lat_count
            rise, fall = up_and_down(face * jnp.where(at_pole, 0.0, 1.0))
            thick = thick_ref[j]
            for i, here in enumerate((thick, tracer_ref[j] * thick)):
                rows = slice(i * level_rows, (i + 1) * level_rows)
                if side:
                    value = partial_ref[j, rows, :lon_count] - (
                        rise * here + fall * row_ref[1 + i, outer]
                    )
                else:
                    value = partial_ref[j, rows, :lon_count] + (
                        rise * row_ref[1 + i, outer] + fall * here
                    )
                moved_ref[j, rows, :lon_count] = value
            to_sectors(send_ref, moved_ref, j, lon_count // send_ref.shape[0])

    @pl.when(polar)
    def _():
        def prepare(j):
            thick = thick_ref[j]
            row_ref[0, j + 1] = v_ref[j].astype(f32)
            row_ref[1, j + 1] = thick
            row_ref[2, j + 1] = tracer_ref[j] * thick
            u_out[j] = u_ref[j]
            v_out[j] = v_ref[j]

        loop(lat_rows, prepare)
        half, quarter, eighth = parts[0][2], parts[1][2], parts[2][2]
        half_wide, quarter_wide, eighth_wide = (padded_to(part[2]) for part in parts[:3])
        last = lat_rows + 2

        def lat_of(g):
            return first_lat + (g if g < lat_rows else g - lat_rows - 1)

        def fold(g, wind):
            real_ref[g, :, lon_count:] = jnp.zeros((level_rows, padded - lon_count), f32)
            real_ref[g, :, :lon_count] = wind
            near = real_ref[g, :, :half_wide]
            far = real_ref[g, :, half : half + half_wide]
            odd, even = near - far, near + far
            work_ref[g, :, :half_wide] = even
            near = even[:, :quarter_wide]
            far = work_ref[g, :, quarter : quarter + quarter_wide]
            two, even = near - far, near + far
            work_ref[g, :, half_wide : half_wide + quarter_wide] = even
            near = even[:, :eighth_wide]
            far = work_ref[g, :, half_wide + eighth : half_wide + eighth + eighth_wide]
            row = jnp.concatenate([odd, two, near - far, near + far], axis=1)
            high = row.astype(bf16).astype(f32)
            both = jnp.concatenate([high, row - high], axis=0)
            split_ref[rows_at(g, 2 * level_rows), :] = both.astype(bf16)

        for j in range(lat_rows):
            fold(j, u_ref[j].astype(f32))
        for j in range(last):
            fold(lat_rows + j, row_ref[0, j])

        for (_, _, _, column), (top, left, size) in zip(parts, places):
            prod_ref[:, column : column + size] = jnp.dot(
                split_ref[:, column : column + size],
                table_ref[top : top + size, left : left + size],
                preferred_element_type=f32,
            )

        for pair in range(groups // 2):
            values = []
            for g in (2 * pair, 2 * pair + 1):
                start = 2 * level_rows * g
                high = prod_ref[start : start + level_rows, :]
                low = prod_ref[start + level_rows : start + 2 * level_rows, :]
                place = jnp.clip(distance(lat_of(g), lat_count), 0, distances - 1)
                values.append((high + low) * damp_ref[place])
            spec_ref[2 * level_rows * pair : 2 * level_rows * (pair + 1), :] = jnp.concatenate(
                values, axis=0
            ).astype(bf16)
        rows = groups * level_rows

        for (_, _, _, column), (top, left, size) in zip(parts, places):
            prod_ref[:rows, column : column + size] = lax.dot_general(
                spec_ref[:, column : column + size],
                table_ref[top : top + size, left : left + size],
                (((1,), (1,)), ((), ())),
                preferred_element_type=f32,
            )

        for g in range(groups):
            start = level_rows * g
            odd, two, four, eight = (
                prod_ref[start : start + level_rows, column : column + padded_to(points)]
                for _, _, points, column in parts
            )
            work_ref[g, :, :eighth_wide] = eight + four
            work_ref[g, :, eighth : 2 * eighth] = (eight - four)[:, :eighth]
            even = work_ref[g, :, :quarter_wide]
            work_ref[g, :, :quarter_wide] = even + two
            work_ref[g, :, quarter : 2 * quarter] = (even - two)[:, :quarter]
            even = work_ref[g, :, :half_wide]
            scale = 1.0 / lon_count
            real_ref[g, :, :half_wide] = (even + odd) * scale
            real_ref[g, :, half : 2 * half] = ((even - odd) * scale)[:, :half]

        def finish(j):
            smooth = real_ref[lat_rows + j, :, :lon_count].astype(bf16)

            @pl.when(is_polar(first_lat + j - 1, lat_count))
            def _():
                row_ref[0, j] = smooth.astype(f32)

                @pl.when(jnp.logical_and(j > 0, j <= lat_rows))
                def _():
                    inner = jnp.clip(j - 1, 0, lat_rows - 1)
                    v_out[inner] = smooth
                    u_out[inner] = real_ref[inner, :, :lon_count].astype(bf16)

        loop(last, finish)

        winds_out = [
            pltpu.make_async_copy(u_out, u_hbm, sems.at[0]),
            pltpu.make_async_copy(v_out, v_hbm, sems.at[1]),
        ]
        for copy in winds_out:
            copy.start()
        least = jnp.where(first_lat == 0, 1, 0)
        most = jnp.where(first_lat + lat_rows == lat_count, lat_rows - 1, lat_rows)

        def advect(j):
            transport(j, u_out, row_ref, real_ref, moved_ref, least, most)
            to_sectors(send_ref, moved_ref, j, lon_count // send_ref.shape[0])

        loop(lat_rows, advect)
        for copy in winds_out:
            copy.wait()


def remap(weight_ref, recv_ref, thick_hbm, tracer_hbm, thick_out, tracer_out, sems):
    lat_rows, level_count, sector = thick_out.shape
    sources, _, wide = recv_ref.shape
    level_rows = level_count // sources
    f32 = jnp.float32
    below, here, above = (weight_ref[place] for place in range(3))
    place = lax.broadcasted_iota(jnp.int32, (level_rows, wide), 0)
    top, bottom = place == 0, place == level_rows - 1

    def results_out(j):
        return [
            pltpu.make_async_copy(source.at[j], target.at[j], sems.at[i, j])
            for i, (source, target) in enumerate(
                ((thick_out, thick_hbm), (tracer_out, tracer_hbm))
            )
        ]

    def work(j):
        blocks = [
            recv_ref[source, rows_at(j, 2 * level_rows), :].astype(f32)
            for source in range(sources)
        ]
        results = []
        for index in range(2):
            layers = [block[level_rows * index : level_rows * (index + 1)] for block in blocks]
            if index == 0:
                layers = [layer + THICK_MID for layer in layers]
            down = [pltpu.roll(layer, 1, 0) for layer in layers]
            up = [pltpu.roll(layer, level_rows - 1, 0) for layer in layers]
            outs = []
            for source in range(sources):
                chosen = slice(level_rows * source, level_rows * (source + 1))
                lower = jnp.where(top, down[max(source - 1, 0)], down[source])
                higher = jnp.where(bottom, up[min(source + 1, sources - 1)], up[source])
                outs.append(
                    below[chosen] * lower + here[chosen] * layers[source] + above[chosen] * higher
                )
            results.append(outs)
        for source in range(sources):
            chosen = slice(level_rows * source, level_rows * (source + 1))
            thick, mass = results[0][source], results[1][source]
            thick_out[j, chosen, :] = thick[:, :sector]
            tracer_out[j, chosen, :] = (mass / thick)[:, :sector]
        for copy in results_out(j):
            copy.start()

    loop(lat_rows, work)
    for j in range(lat_rows):
        for copy in results_out(j):
            copy.wait()


def per_device(u_wind, v_wind, thickness, tracer, remap_index, remap_frac):
    lat_rows, level_rows, lon_count = u_wind.shape
    lat_devices = lax.axis_size("lat")
    lat_count = lat_rows * lat_devices
    sectors = lax.axis_size("lev")
    level_count = level_rows * sectors
    sector = lon_count // sectors
    sector_wide = padded_to(sector)
    tables, damping = filter_tables(lat_count, lon_count)
    columns = damping.shape[2]
    padded = (lon_count // LANES + 2) * LANES
    f32, bf16 = jnp.float32, jnp.bfloat16

    in_hbm = pl.BlockSpec(memory_space=pltpu.HBM)
    in_vmem = pl.BlockSpec(memory_space=pltpu.VMEM)

    def limit(mebibytes):
        return pltpu.CompilerParams(vmem_limit_bytes=mebibytes * 1024 * 1024)

    edges = (3, level_rows, lon_count)

    def stay(array):
        return pltpu.with_memory_space_constraint(jnp.asarray(array), pltpu.HBM)

    near, beyond = pl.pallas_call(
        pack,
        out_shape=(pltpu.VMEM(edges, bf16), pltpu.VMEM(edges, bf16)),
        in_specs=[in_hbm] * 3,
        out_specs=(in_vmem, in_vmem),
        scratch_shapes=[
            pltpu.VMEM((2, level_rows, lon_count), bf16),
            pltpu.VMEM((2, level_rows, lon_count), f32),
            pltpu.VMEM((2, level_rows, lon_count), f32),
            pltpu.SemaphoreType.DMA((6,)),
        ],
        compiler_params=limit(8),
        name="pack",
    )(*(stay(array) for array in (v_wind, thickness, tracer)))
    swap_near = [(i, i ^ 1) for i in range(lat_devices)]
    swap_next = [(i, i - 1 + 2 * (i % 2)) for i in range(1, lat_devices - 1)]
    near = lax.ppermute(near, "lat", swap_near)
    beyond = lax.ppermute(beyond, "lat", swap_next)

    arrays = (u_wind, v_wind, thickness, tracer, tables, damping)
    moved_bytes = sum(array.size * array.dtype.itemsize for array in arrays)
    send_shape = (sectors, 2 * lat_rows * level_rows, sector_wide)
    moved_shape = (lat_rows, 2 * level_rows, padded)
    held = (pltpu.HBM(u_wind.shape, bf16), pltpu.HBM(v_wind.shape, bf16), pltpu.VMEM(send_shape, bf16))
    in_held = [in_hbm, in_hbm, in_vmem]
    rows_shape = (3, lat_rows + 2, level_rows, lon_count)
    *loaded, u_filtered, v_filtered, send, moved, weights = pl.pallas_call(
        functools.partial(load, lat_count),
        out_shape=[pltpu.VMEM(array.shape, array.dtype) for array in arrays]
        + [*held, pltpu.VMEM(moved_shape, f32), pltpu.VMEM((3, level_count, sector_wide), f32)],
        in_specs=[in_hbm] * (2 + len(arrays)),
        out_specs=[in_vmem] * len(arrays) + in_held + [in_vmem] * 2,
        scratch_shapes=[
            pltpu.VMEM(rows_shape, f32),
            pltpu.VMEM((3, level_rows, padded), f32),
            pltpu.SMEM(remap_index.shape, jnp.int32),
            pltpu.SMEM(remap_frac.shape, f32),
            pltpu.SemaphoreType.DMA((9,)),
            pltpu.SemaphoreType.DMA((4,)),
        ],
        compiler_params=limit(8),
        cost_estimate=pl.CostEstimate(flops=0, bytes_accessed=moved_bytes, transcendentals=0),
        name="load",
    )(*(stay(array) for array in (remap_index, remap_frac, *arrays)))
    groups = 2 * lat_rows + 2
    before_held = len(loaded) + 3
    u_filtered, v_filtered, send = pl.pallas_call(
        functools.partial(filter_advect, lat_count),
        out_shape=held,
        in_specs=[in_vmem] * before_held + in_held,
        out_specs=tuple(in_held),
        input_output_aliases={before_held + i: i for i in range(3)},
        scratch_shapes=[
            pltpu.VMEM(u_wind.shape, bf16),
            pltpu.VMEM(v_wind.shape, bf16),
            pltpu.VMEM((groups, level_rows, padded), f32),
            pltpu.VMEM((groups, level_rows, padded), f32),
            pltpu.VMEM((2 * groups * level_rows, columns), bf16),
            pltpu.VMEM((2 * groups * level_rows, columns), f32),
            pltpu.VMEM((groups * level_rows, columns), bf16),
            pltpu.VMEM(rows_shape, f32),
            pltpu.VMEM(moved_shape, f32),
            pltpu.SemaphoreType.DMA((2,)),
        ],
        compiler_params=limit(20),
        name="filter_advect",
    )(*loaded, moved, near, beyond, u_filtered, v_filtered, send)
    recv = lax.all_to_all(send, "lev", split_axis=0, concat_axis=0, tiled=True)
    shape = (lat_rows, level_count, sector)
    thick_out, tracer_out = pl.pallas_call(
        remap,
        out_shape=(pltpu.HBM(shape, f32), pltpu.HBM(shape, f32)),
        in_specs=[in_vmem] * 2,
        out_specs=(in_hbm, in_hbm),
        scratch_shapes=[
            pltpu.VMEM(shape, f32),
            pltpu.VMEM(shape, f32),
            pltpu.SemaphoreType.DMA((2, lat_rows)),
        ],
        compiler_params=limit(8),
        name="remap",
    )(weights, recv)
    return u_filtered, v_filtered, thick_out, tracer_out


def solution(mesh):
    placed = (
        P("lat", "lev", None),
        P("lat", "lev", None),
        P("lat", "lev", None),
        P("lat", "lev", None),
        P(),
        P(),
    )
    return jax.shard_map(
        per_device,
        mesh=mesh,
        in_specs=placed,
        out_specs=(
            P("lat", "lev", None),
            P("lat", "lev", None),
            P("lat", None, "lev"),
            P("lat", None, "lev"),
        ),
        check_vma=False,
    )
```

```python
import functools
import math

import jax
import jax.numpy as jnp
import ml_dtypes
import numpy as np
from jax import lax
from jax.experimental import pallas as pl
from jax.experimental.pallas import tpu as pltpu
from jax.sharding import PartitionSpec as P

COS_EDGE = math.cos(66.0 * math.pi / 180.0)
LANES = 128
THICK_MID = 1.25


def padded_to(count):
    return -(-count // LANES) * LANES


def filter_parts(lon_count):
    parts = []
    column = 0
    for first, step, points in (
        (1, 2, lon_count // 2),
        (2, 4, lon_count // 4),
        (4, 8, lon_count // 8),
        (0, 8, lon_count // 8),
    ):
        parts.append((first, step, points, column))
        column += padded_to(points)
    return parts, column


def table_places(parts):
    odd, two, four, eight = (padded_to(part[2]) for part in parts)
    return [(0, 0, odd), (0, odd, two), (two, odd, four), (two, odd + four, eight)]


def filter_tables(lat_count, lon_count):
    phase = 2.0 * np.pi * np.arange(lon_count) / lon_count
    rounded = (np.cos(phase) + np.sin(phase)).astype(np.float32).astype(ml_dtypes.bfloat16)
    polar = [d for d in range((lat_count + 1) // 2) if 15 * d < 2 * (lat_count - 1)]
    ratio = (np.sin(np.pi * np.array(polar, np.float64) / (lat_count - 1)) / COS_EDGE) ** 2
    wave = np.arange(lon_count)
    wave = np.minimum(wave, lon_count - wave)
    sine_square = np.sin(np.pi * wave / lon_count) ** 2
    sine_square[0] = 1.0
    values = np.minimum(1.0, ratio[:, None] / sine_square[None, :])
    values[:, 0] = 1.0

    parts, columns = filter_parts(lon_count)
    places = table_places(parts)
    tables = np.zeros((places[0][2], places[0][2] + places[1][2]), ml_dtypes.bfloat16)
    damping = np.zeros((len(polar), 1, columns), np.float32)
    for (first, step, points, column), (row, left, _) in zip(parts, places):
        waves = first + step * np.arange(points)
        values_here = rounded[np.arange(points)[:, None] * waves[None, :] % lon_count]
        tables[row : row + points, left : left + points] = values_here
        damping[:, 0, column : column + points] = values[:, waves]
    return tables, damping


def distance(lat, lat_count):
    return jnp.minimum(lat, lat_count - 1 - lat)


def is_polar(lat, lat_count):
    d = distance(lat, lat_count)
    return jnp.logical_and(d >= 0, 15 * d < 2 * (lat_count - 1))


def band_is_polar(first_lat, lat_rows, lat_count):
    found = is_polar(first_lat, lat_count)
    for offset in (-1, lat_rows - 1, lat_rows):
        found = jnp.logical_or(found, is_polar(first_lat + offset, lat_count))
    return found


def pack(v_hbm, thick_hbm, tracer_hbm, near_out, next_out, v_buf, thick_buf, tracer_buf, sems):
    lat_rows = v_hbm.shape[0]
    copies = []
    for side, row in enumerate((0, lat_rows - 1)):
        for source, target in ((v_hbm, v_buf), (thick_hbm, thick_buf), (tracer_hbm, tracer_buf)):
            copy = pltpu.make_async_copy(source.at[row], target.at[side], sems.at[len(copies)])
            copy.start()
            copies.append(copy)
    for copy in copies:
        copy.wait()
    odd = lax.axis_index("lat") % 2
    for out, side in ((near_out, 1 - odd), (next_out, odd)):
        thick = thick_buf[side]
        out[0] = v_buf[side]
        out[1] = thick.astype(jnp.bfloat16)
        out[2] = (tracer_buf[side] * thick).astype(jnp.bfloat16)


def courant(wind):
    return jnp.clip(0.05 * wind, -0.15, 0.15)


def loop(count, body, unroll=1):
    def step(place, carry):
        body(place)
        return carry

    lax.fori_loop(0, count, step, 0, unroll=unroll)


def rows_at(place, count):
    return pl.ds(pl.multiple_of(place * count, count), count)


def up_and_down(face):
    return jnp.maximum(face, 0.0), jnp.minimum(face, 0.0)


def to_sectors(send_ref, moved_ref, j, sector):
    sectors, _, sector_wide = send_ref.shape
    height = moved_ref.shape[1]
    for s in range(sectors):
        block = moved_ref[j, :, s * sector : s * sector + sector_wide]
        send_ref[s, rows_at(j, height), :] = block.astype(send_ref.dtype)


def transport(j, wind_ref, row_ref, real_ref, moved_ref, least_face, most_face):
    level_rows, lon_count = row_ref.shape[2:]
    padded = real_ref.shape[2]
    whole = lon_count // LANES * LANES
    rest = lon_count - whole
    lane = lax.broadcasted_iota(jnp.int32, (level_rows, LANES), 1)

    def extend(index, value):
        real_ref[index, :, :lon_count] = value
        tail = jnp.where(
            lane < rest,
            real_ref[index, :, whole : whole + LANES],
            pltpu.roll(real_ref[index, :, :LANES], rest, 1),
        )
        ends = pltpu.roll(tail, LANES - rest, 1)
        real_ref[index, :, whole : whole + LANES] = tail
        real_ref[index, :, whole + LANES :] = ends
        return real_ref[index]

    def before(value):
        return pltpu.roll(value, 1, 1)

    def after(value):
        return pltpu.roll(value, padded - 1, 1)

    def face_y(f):
        face = 0.5 * (courant(row_ref[0, f]) + courant(row_ref[0, f + 1]))
        inside = jnp.logical_and(f >= least_face, f <= most_face)
        return up_and_down(face * jnp.where(inside, 1.0, 0.0))

    (rise_below, fall_below), (rise_above, fall_above) = face_y(j), face_y(j + 1)
    courant_x = extend(3 * (j % 2), courant(wind_ref[j].astype(jnp.float32)))
    rise_x, fall_x = up_and_down(0.5 * (before(courant_x) + courant_x))
    for i in range(2):
        below, here, above = (row_ref[1 + i, j + k] for k in range(3))
        field = extend(3 * (j % 2) + 1 + i, here)
        flux_x = rise_x * before(field) + fall_x * field
        across = rise_above * here + fall_above * above - rise_below * below - fall_below * here
        result = field - (after(flux_x) - flux_x)
        if i == 0:
            result = result - THICK_MID
        moved_ref[j, i * level_rows : (i + 1) * level_rows, :lon_count] = (
            result[:, :lon_count] - across
        )


def band_weights(index_ref, frac_ref, weight_ref):
    _, level_count, wide = weight_ref.shape

    def inner(k):
        return jnp.where(index_ref[k] == k, 1.0, frac_ref[k])

    def outer(k):
        return jnp.where(index_ref[k] == k, frac_ref[k], 0.0)

    def weigh(k):
        for place, weight in enumerate(
            (1.0 - inner(k), inner(k + 1) - outer(k), outer(k + 1))
        ):
            weight_ref[place, pl.ds(k, 1), :] = jnp.full((1, wide), weight, jnp.float32)

    loop(level_count, weigh)


def fold(wind, slot, slot_ref, work_ref, split_ref, rows):
    level_rows, lon_count = wind.shape
    padded = slot_ref.shape[2]
    parts, _ = filter_parts(lon_count)
    half, quarter, eighth = (part[2] for part in parts[:3])
    half_wide, quarter_wide, eighth_wide = (padded_to(part[2]) for part in parts[:3])
    slot_ref[slot, :, lon_count:] = jnp.zeros((level_rows, padded - lon_count), jnp.float32)
    slot_ref[slot, :, :lon_count] = wind
    near = slot_ref[slot, :, :half_wide]
    far = slot_ref[slot, :, half : half + half_wide]
    odd, even = near - far, near + far
    work_ref[slot, :, :half_wide] = even
    near = even[:, :quarter_wide]
    far = work_ref[slot, :, quarter : quarter + quarter_wide]
    two, even = near - far, near + far
    work_ref[slot, :, half_wide : half_wide + quarter_wide] = even
    near = even[:, :eighth_wide]
    far = work_ref[slot, :, half_wide + eighth : half_wide + eighth + eighth_wide]
    row = jnp.concatenate([odd, two, near - far, near + far], axis=1)
    high = row.astype(jnp.bfloat16).astype(jnp.float32)
    both = jnp.concatenate([high, row - high], axis=0)
    split_ref[rows, :] = both.astype(jnp.bfloat16)


def load(
    lat_count,
    index_hbm,
    frac_hbm,
    u_hbm,
    v_hbm,
    thick_hbm,
    tracer_hbm,
    table_hbm,
    damp_hbm,
    u_ref,
    v_ref,
    thick_ref,
    tracer_ref,
    table_ref,
    damp_ref,
    turned_ref,
    u_out,
    v_out,
    send_ref,
    split_ref,
    moved_ref,
    weight_ref,
    row_ref,
    real_ref,
    work_ref,
    index_ref,
    frac_ref,
    sems,
    table_sems,
):
    lat_rows, level_rows, lon_count = u_ref.shape
    f32 = jnp.float32
    polar = band_is_polar(lax.axis_index("lat") * lat_rows, lat_rows, lat_count)
    inputs = [
        pltpu.make_async_copy(source, target, sems.at[place])
        for place, (source, target) in enumerate(
            ((v_hbm, v_ref), (thick_hbm, thick_ref), (tracer_hbm, tracer_ref), (u_hbm, u_ref))
        )
    ]
    tables = [pltpu.make_async_copy(damp_hbm, damp_ref, sems.at[4])]
    parts, _ = filter_parts(lon_count)
    places = table_places(parts)
    points, split_at, columns = parts[0][2], places[0][2], table_hbm.shape[1]
    upper = places[2][0] + places[2][2]
    chunks = table_sems.shape[0] - 1
    height = upper // chunks

    def table_copy(chunk):
        if isinstance(chunk, int) and chunk == chunks:
            part = (pl.ds(upper, points - upper), pl.ds(0, split_at))
        else:
            part = (rows_at(chunk, height), pl.ds(0, columns))
        return pltpu.make_async_copy(
            table_hbm.at[part], table_ref.at[part], table_sems.at[chunk]
        )

    tables += [table_copy(chunk) for chunk in range(chunks + 1)]
    for copy in inputs:
        copy.start()

    @pl.when(polar)
    def _():
        for copy in tables:
            copy.start()

    scalars = [
        pltpu.make_async_copy(index_hbm, index_ref, sems.at[7]),
        pltpu.make_async_copy(frac_hbm, frac_ref, sems.at[8]),
    ]
    for copy in scalars:
        copy.start()

    def weigh():
        for copy in scalars:
            copy.wait()
        band_weights(index_ref, frac_ref, weight_ref)

    @pl.when(polar)
    def _():
        weigh()
        for copy in inputs:
            copy.wait()
        slots = real_ref.shape[0]
        for g in range(2 * lat_rows):
            wind = (u_ref if g < lat_rows else v_ref)[g % lat_rows].astype(f32)
            rows = slice(2 * level_rows * g, 2 * level_rows * (g + 1))
            fold(wind, g % slots, real_ref, work_ref, split_ref, rows)
        table_ref[points:split_at, :split_at] = jnp.zeros((split_at - points, split_at), jnp.bfloat16)
        for chunk in range(chunks + 1):
            table_copy(chunk).wait()
            start, stop = chunk * height, (chunk + 1) * height
            for top, left, size in places:
                low, high = max(start, top), min(stop, top + size)
                if low < high:
                    turned_ref[top : top + size, left + low - top : left + high - top] = (
                        table_ref[low:high, left : left + size].T
                    )
        tables[0].wait()

    @pl.when(jnp.logical_not(polar))
    def _():
        for copy in inputs:
            copy.wait()
        winds = [
            pltpu.make_async_copy(u_ref, u_out, sems.at[5]),
            pltpu.make_async_copy(v_ref, v_out, sems.at[6]),
        ]
        for copy in winds:
            copy.start()
        blank = jnp.zeros((level_rows, lon_count), f32)
        for place in range(3):
            row_ref[place, 0] = blank
            row_ref[place, lat_rows + 1] = blank

        def prepare(j):
            thick = thick_ref[j]
            row_ref[0, j + 1] = v_ref[j].astype(f32)
            row_ref[1, j + 1] = thick
            row_ref[2, j + 1] = tracer_ref[j] * thick

        loop(lat_rows, prepare)

        def advect(j):
            transport(j, u_ref, row_ref, real_ref, moved_ref, 1, lat_rows - 1)

            @pl.when(jnp.logical_and(j > 0, j < lat_rows - 1))
            def _():
                to_sectors(send_ref, moved_ref, j, lon_count // send_ref.shape[0])

        loop(lat_rows, advect, 2)
        weigh()
        for copy in winds:
            copy.wait()


def filter_advect(
    lat_count,
    u_ref,
    v_ref,
    thick_ref,
    tracer_ref,
    table_ref,
    damp_ref,
    turned_ref,
    partial_ref,
    next_ref,
    near_ref,
    u_held,
    v_held,
    send_held,
    split_held,
    u_hbm,
    v_hbm,
    send_ref,
    split_ref,
    u_out,
    v_out,
    real_ref,
    work_ref,
    prod_ref,
    spec_ref,
    row_ref,
    moved_ref,
    sems,
):
    lat_rows, level_rows, lon_count = u_ref.shape
    groups, _, padded = real_ref.shape
    distances = damp_ref.shape[0]
    first_lat = lax.axis_index("lat") * lat_rows
    f32 = jnp.float32
    bf16 = jnp.bfloat16
    parts, columns = filter_parts(lon_count)
    places = table_places(parts)
    odd_device = lax.axis_index("lat") % 2
    polar = band_is_polar(first_lat, lat_rows, lat_count)

    for side in range(2):
        for source, odd in ((near_ref, 1 - side), (next_ref, side)):

            @pl.when(odd_device == odd)
            def _():
                for place in range(3):
                    row_ref[place, side * (lat_rows + 1)] = source[place].astype(f32)

    @pl.when(jnp.logical_not(polar))
    def _():
        for side, j in enumerate((0, lat_rows - 1)):
            outer = side * (lat_rows + 1)
            own = courant(v_ref[j].astype(f32))
            face = 0.5 * (courant(row_ref[0, outer]) + own)
            at_pole = first_lat + side * lat_rows == side * lat_count
            rise, fall = up_and_down(face * jnp.where(at_pole, 0.0, 1.0))
            thick = thick_ref[j]
            for i, here in enumerate((thick, tracer_ref[j] * thick)):
                rows = slice(i * level_rows, (i + 1) * level_rows)
                if side:
                    value = partial_ref[j, rows, :lon_count] - (
                        rise * here + fall * row_ref[1 + i, outer]
                    )
                else:
                    value = partial_ref[j, rows, :lon_count] + (
                        rise * row_ref[1 + i, outer] + fall * here
                    )
                moved_ref[j, rows, :lon_count] = value
            to_sectors(send_ref, moved_ref, j, lon_count // send_ref.shape[0])

    @pl.when(polar)
    def _():
        def prepare(j):
            thick = thick_ref[j]
            row_ref[0, j + 1] = v_ref[j].astype(f32)
            row_ref[1, j + 1] = thick
            row_ref[2, j + 1] = tracer_ref[j] * thick
            u_out[j] = u_ref[j]
            v_out[j] = v_ref[j]

        loop(lat_rows, prepare)
        half, quarter, eighth = (part[2] for part in parts[:3])
        half_wide, quarter_wide, eighth_wide = (padded_to(part[2]) for part in parts[:3])

        def lat_of(g):
            if g < 2 * lat_rows:
                return first_lat + g % lat_rows
            return first_lat + (lat_rows if g % 2 else -1)

        for side in range(2):
            g = 2 * lat_rows + side
            rows = slice(2 * level_rows * g, 2 * level_rows * (g + 1))
            wind = row_ref[0, side * (lat_rows + 1)]
            fold(wind, side, real_ref, work_ref, split_ref, rows)

        for (_, _, _, column), (top, left, size) in zip(parts, places):
            prod_ref[:, column : column + size] = jnp.dot(
                split_ref[:, column : column + size],
                table_ref[top : top + size, left : left + size],
                preferred_element_type=f32,
            )

        for pair in range(groups // 2):
            values = []
            for g in (2 * pair, 2 * pair + 1):
                start = 2 * level_rows * g
                high = prod_ref[start : start + level_rows, :]
                low = prod_ref[start + level_rows : start + 2 * level_rows, :]
                place = jnp.clip(distance(lat_of(g), lat_count), 0, distances - 1)
                values.append((high + low) * damp_ref[place])
            spec_ref[2 * level_rows * pair : 2 * level_rows * (pair + 1), :] = jnp.concatenate(
                values, axis=0
            ).astype(bf16)
        rows = groups * level_rows

        for (_, _, _, column), (top, left, size) in zip(parts, places):
            prod_ref[:rows, column : column + size] = jnp.dot(
                spec_ref[:, column : column + size],
                turned_ref[top : top + size, left : left + size],
                preferred_element_type=f32,
            )

        for g in range(groups):
            start = level_rows * g
            odd, two, four, eight = (
                prod_ref[start : start + level_rows, column : column + padded_to(points)]
                for _, _, points, column in parts
            )
            work_ref[g, :, :eighth_wide] = eight + four
            work_ref[g, :, eighth : 2 * eighth] = (eight - four)[:, :eighth]
            even = work_ref[g, :, :quarter_wide]
            work_ref[g, :, :quarter_wide] = even + two
            work_ref[g, :, quarter : 2 * quarter] = (even - two)[:, :quarter]
            even = work_ref[g, :, :half_wide]
            scale = 1.0 / lon_count
            real_ref[g, :, :half_wide] = (even + odd) * scale
            real_ref[g, :, half : 2 * half] = ((even - odd) * scale)[:, :half]

        def finish(j):
            @pl.when(is_polar(first_lat + j, lat_count))
            def _():
                u_out[j] = real_ref[j, :, :lon_count].astype(bf16)
                smooth = real_ref[lat_rows + j, :, :lon_count].astype(bf16)
                v_out[j] = smooth
                row_ref[0, j + 1] = smooth.astype(f32)

        loop(lat_rows, finish)
        for side in range(2):

            @pl.when(is_polar(lat_of(2 * lat_rows + side), lat_count))
            def _():
                smooth = real_ref[2 * lat_rows + side, :, :lon_count].astype(bf16)
                row_ref[0, side * (lat_rows + 1)] = smooth.astype(f32)

        winds_out = [
            pltpu.make_async_copy(u_out, u_hbm, sems.at[0]),
            pltpu.make_async_copy(v_out, v_hbm, sems.at[1]),
        ]
        for copy in winds_out:
            copy.start()
        least = jnp.where(first_lat == 0, 1, 0)
        most = jnp.where(first_lat + lat_rows == lat_count, lat_rows - 1, lat_rows)

        def advect(j):
            transport(j, u_out, row_ref, real_ref, moved_ref, least, most)
            to_sectors(send_ref, moved_ref, j, lon_count // send_ref.shape[0])

        loop(lat_rows, advect, 2)
        for copy in winds_out:
            copy.wait()


def remap(weight_ref, recv_ref, thick_hbm, tracer_hbm, thick_out, tracer_out, sems):
    lat_rows, level_count, sector = thick_out.shape
    sources, _, wide = recv_ref.shape
    level_rows = level_count // sources
    f32 = jnp.float32
    below, here, above = (weight_ref[place] for place in range(3))
    place = lax.broadcasted_iota(jnp.int32, (level_rows, wide), 0)
    top, bottom = place == 0, place == level_rows - 1

    def results_out(j):
        return [
            pltpu.make_async_copy(source.at[j], target.at[j], sems.at[i, j])
            for i, (source, target) in enumerate(
                ((thick_out, thick_hbm), (tracer_out, tracer_hbm))
            )
        ]

    def work(j):
        blocks = [
            recv_ref[source, rows_at(j, 2 * level_rows), :].astype(f32)
            for source in range(sources)
        ]
        results = []
        for index in range(2):
            layers = [block[level_rows * index : level_rows * (index + 1)] for block in blocks]
            if index == 0:
                layers = [layer + THICK_MID for layer in layers]
            down = [pltpu.roll(layer, 1, 0) for layer in layers]
            up = [pltpu.roll(layer, level_rows - 1, 0) for layer in layers]
            outs = []
            for source in range(sources):
                chosen = slice(level_rows * source, level_rows * (source + 1))
                lower = jnp.where(top, down[max(source - 1, 0)], down[source])
                higher = jnp.where(bottom, up[min(source + 1, sources - 1)], up[source])
                outs.append(
                    below[chosen] * lower + here[chosen] * layers[source] + above[chosen] * higher
                )
            results.append(outs)
        for source in range(sources):
            chosen = slice(level_rows * source, level_rows * (source + 1))
            thick, mass = results[0][source], results[1][source]
            thick_out[j, chosen, :] = thick[:, :sector]
            tracer_out[j, chosen, :] = (mass / thick)[:, :sector]
        for copy in results_out(j):
            copy.start()

    loop(lat_rows, work)
    for j in range(lat_rows):
        for copy in results_out(j):
            copy.wait()


def per_device(u_wind, v_wind, thickness, tracer, remap_index, remap_frac):
    lat_rows, level_rows, lon_count = u_wind.shape
    lat_devices = lax.axis_size("lat")
    lat_count = lat_rows * lat_devices
    sectors = lax.axis_size("lev")
    level_count = level_rows * sectors
    sector = lon_count // sectors
    sector_wide = padded_to(sector)
    tables, damping = filter_tables(lat_count, lon_count)
    columns = damping.shape[2]
    padded = (lon_count // LANES + 2) * LANES
    f32, bf16 = jnp.float32, jnp.bfloat16

    in_hbm = pl.BlockSpec(memory_space=pltpu.HBM)
    in_vmem = pl.BlockSpec(memory_space=pltpu.VMEM)

    def limit(mebibytes):
        return pltpu.CompilerParams(vmem_limit_bytes=mebibytes * 1024 * 1024)

    edges = (3, level_rows, lon_count)

    def stay(array):
        return pltpu.with_memory_space_constraint(jnp.asarray(array), pltpu.HBM)

    near, beyond = pl.pallas_call(
        pack,
        out_shape=(pltpu.VMEM(edges, bf16), pltpu.VMEM(edges, bf16)),
        in_specs=[in_hbm] * 3,
        out_specs=(in_vmem, in_vmem),
        scratch_shapes=[
            pltpu.VMEM((2, level_rows, lon_count), bf16),
            pltpu.VMEM((2, level_rows, lon_count), f32),
            pltpu.VMEM((2, level_rows, lon_count), f32),
            pltpu.SemaphoreType.DMA((6,)),
        ],
        compiler_params=limit(8),
        name="pack",
    )(*(stay(array) for array in (v_wind, thickness, tracer)))
    swap_near = [(i, i ^ 1) for i in range(lat_devices)]
    swap_next = [(i, i - 1 + 2 * (i % 2)) for i in range(1, lat_devices - 1)]
    near = lax.ppermute(near, "lat", swap_near)
    beyond = lax.ppermute(beyond, "lat", swap_next)

    arrays = (u_wind, v_wind, thickness, tracer, tables, damping)
    moved_bytes = sum(array.size * array.dtype.itemsize for array in arrays)
    send_shape = (sectors, 2 * lat_rows * level_rows, sector_wide)
    moved_shape = (lat_rows, 2 * level_rows, padded)
    groups = 2 * lat_rows + 2
    held = (
        pltpu.HBM(u_wind.shape, bf16),
        pltpu.HBM(v_wind.shape, bf16),
        pltpu.VMEM(send_shape, bf16),
        pltpu.VMEM((2 * groups * level_rows, columns), bf16),
    )
    in_held = [in_hbm, in_hbm, in_vmem, in_vmem]
    rows_shape = (3, lat_rows + 2, level_rows, lon_count)
    *loaded, u_filtered, v_filtered, send, split, moved, weights = pl.pallas_call(
        functools.partial(load, lat_count),
        out_shape=[pltpu.VMEM(array.shape, array.dtype) for array in (*arrays, tables)]
        + [*held, pltpu.VMEM(moved_shape, f32), pltpu.VMEM((3, level_count, sector_wide), f32)],
        in_specs=[in_hbm] * (2 + len(arrays)),
        out_specs=[in_vmem] * (len(arrays) + 1) + in_held + [in_vmem] * 2,
        scratch_shapes=[
            pltpu.VMEM(rows_shape, f32),
            pltpu.VMEM((6, level_rows, padded), f32),
            pltpu.VMEM((6, level_rows, padded), f32),
            pltpu.SMEM(remap_index.shape, jnp.int32),
            pltpu.SMEM(remap_frac.shape, f32),
            pltpu.SemaphoreType.DMA((9,)),
            pltpu.SemaphoreType.DMA((4,)),
        ],
        compiler_params=limit(8),
        cost_estimate=pl.CostEstimate(flops=0, bytes_accessed=moved_bytes, transcendentals=0),
        name="load",
    )(*(stay(array) for array in (remap_index, remap_frac, *arrays)))
    before_held = len(loaded) + 3
    u_filtered, v_filtered, send, _ = pl.pallas_call(
        functools.partial(filter_advect, lat_count),
        out_shape=held,
        in_specs=[in_vmem] * before_held + in_held,
        out_specs=tuple(in_held),
        input_output_aliases={before_held + i: i for i in range(4)},
        scratch_shapes=[
            pltpu.VMEM(u_wind.shape, bf16),
            pltpu.VMEM(v_wind.shape, bf16),
            pltpu.VMEM((groups, level_rows, padded), f32),
            pltpu.VMEM((groups, level_rows, padded), f32),
            pltpu.VMEM((2 * groups * level_rows, columns), f32),
            pltpu.VMEM((groups * level_rows, columns), bf16),
            pltpu.VMEM(rows_shape, f32),
            pltpu.VMEM(moved_shape, f32),
            pltpu.SemaphoreType.DMA((2,)),
        ],
        compiler_params=limit(20),
        name="filter_advect",
    )(*loaded, moved, beyond, near, u_filtered, v_filtered, send, split)
    recv = lax.all_to_all(send, "lev", split_axis=0, concat_axis=0, tiled=True)
    shape = (lat_rows, level_count, sector)
    thick_out, tracer_out = pl.pallas_call(
        remap,
        out_shape=(pltpu.HBM(shape, f32), pltpu.HBM(shape, f32)),
        in_specs=[in_vmem] * 2,
        out_specs=(in_hbm, in_hbm),
        scratch_shapes=[
            pltpu.VMEM(shape, f32),
            pltpu.VMEM(shape, f32),
            pltpu.SemaphoreType.DMA((2, lat_rows)),
        ],
        compiler_params=limit(8),
        name="remap",
    )(weights, recv)
    return u_filtered, v_filtered, thick_out, tracer_out


def solution(mesh):
    placed = (
        P("lat", "lev", None),
        P("lat", "lev", None),
        P("lat", "lev", None),
        P("lat", "lev", None),
        P(),
        P(),
    )
    return jax.shard_map(
        per_device,
        mesh=mesh,
        in_specs=placed,
        out_specs=(
            P("lat", "lev", None),
            P("lat", "lev", None),
            P("lat", None, "lev"),
            P("lat", None, "lev"),
        ),
        check_vma=False,
    )
```

```python
import functools
import math

import jax
import jax.numpy as jnp
import ml_dtypes
import numpy as np
from jax import lax
from jax.experimental import pallas as pl
from jax.experimental.pallas import tpu as pltpu
from jax.sharding import PartitionSpec as P

COS_EDGE = math.cos(66.0 * math.pi / 180.0)
LANES = 128
THICK_MID = 1.0


def padded_to(count):
    return -(-count // LANES) * LANES


def filter_parts(lon_count):
    parts = []
    column = 0
    for first, step, points in (
        (1, 2, lon_count // 2),
        (2, 4, lon_count // 4),
        (4, 8, lon_count // 8),
        (0, 8, lon_count // 8),
    ):
        parts.append((first, step, points, column))
        column += padded_to(points)
    return parts, column


def table_places(parts):
    odd, two, four, eight = (padded_to(part[2]) for part in parts)
    return [(0, 0, odd), (0, odd, two), (two, odd, four), (two, odd + four, eight)]


def filter_tables(lat_count, lon_count):
    phase = 2.0 * np.pi * np.arange(lon_count) / lon_count
    rounded = (np.cos(phase) + np.sin(phase)).astype(np.float32).astype(ml_dtypes.bfloat16)
    polar = [d for d in range((lat_count + 1) // 2) if 15 * d < 2 * (lat_count - 1)]
    ratio = (np.sin(np.pi * np.array(polar, np.float64) / (lat_count - 1)) / COS_EDGE) ** 2
    wave = np.arange(lon_count)
    wave = np.minimum(wave, lon_count - wave)
    sine_square = np.sin(np.pi * wave / lon_count) ** 2
    sine_square[0] = 1.0
    values = np.minimum(1.0, ratio[:, None] / sine_square[None, :])
    values[:, 0] = 1.0

    parts, columns = filter_parts(lon_count)
    places = table_places(parts)
    tables = np.zeros((places[0][2], places[0][2] + places[1][2]), ml_dtypes.bfloat16)
    damping = np.zeros((len(polar), 1, columns), np.float32)
    for (first, step, points, column), (row, left, _) in zip(parts, places):
        waves = first + step * np.arange(points)
        values_here = rounded[np.arange(points)[:, None] * waves[None, :] % lon_count]
        tables[row : row + points, left : left + points] = values_here
        damping[:, 0, column : column + points] = values[:, waves]
    return tables, damping


def distance(lat, lat_count):
    return jnp.minimum(lat, lat_count - 1 - lat)


def is_polar(lat, lat_count):
    d = distance(lat, lat_count)
    return jnp.logical_and(d >= 0, 15 * d < 2 * (lat_count - 1))


def band_is_polar(first_lat, lat_rows, lat_count):
    found = is_polar(first_lat, lat_count)
    for offset in (-1, lat_rows - 1, lat_rows):
        found = jnp.logical_or(found, is_polar(first_lat + offset, lat_count))
    return found


def pack(v_hbm, thick_hbm, tracer_hbm, near_out, next_out, v_buf, thick_buf, tracer_buf, sems):
    lat_rows = v_hbm.shape[0]
    copies = []
    for side, row in enumerate((0, lat_rows - 1)):
        for source, target in ((v_hbm, v_buf), (thick_hbm, thick_buf), (tracer_hbm, tracer_buf)):
            copy = pltpu.make_async_copy(source.at[row], target.at[side], sems.at[len(copies)])
            copy.start()
            copies.append(copy)
    for copy in copies:
        copy.wait()
    odd = lax.axis_index("lat") % 2
    for out, side in ((near_out, 1 - odd), (next_out, odd)):
        thick = thick_buf[side]
        out[0] = v_buf[side]
        out[1] = thick.astype(jnp.bfloat16)
        out[2] = (tracer_buf[side] * thick).astype(jnp.bfloat16)


def courant(wind):
    return jnp.clip(0.05 * wind, -0.15, 0.15)


def loop(count, body, unroll=1):
    def step(place, carry):
        body(place)
        return carry

    lax.fori_loop(0, count, step, 0, unroll=unroll)


def rows_at(place, count):
    return pl.ds(pl.multiple_of(place * count, count), count)


def up_and_down(face):
    return jnp.maximum(face, 0.0), jnp.minimum(face, 0.0)


def to_sectors(send_ref, moved_ref, j, sector):
    sectors, _, sector_wide = send_ref.shape
    height = moved_ref.shape[1]
    for s in range(sectors):
        block = moved_ref[j, :, s * sector : s * sector + sector_wide]
        send_ref[s, rows_at(j, height), :] = block.astype(send_ref.dtype)


def transport(j, wind_ref, row_ref, real_ref, moved_ref, least_face, most_face):
    level_rows, lon_count = row_ref.shape[2:]
    padded = real_ref.shape[2]
    whole = lon_count // LANES * LANES
    rest = lon_count - whole
    lane = lax.broadcasted_iota(jnp.int32, (level_rows, LANES), 1)

    def extend(index, value):
        real_ref[index, :, :lon_count] = value
        tail = jnp.where(
            lane < rest,
            real_ref[index, :, whole : whole + LANES],
            pltpu.roll(real_ref[index, :, :LANES], rest, 1),
        )
        ends = pltpu.roll(tail, LANES - rest, 1)
        real_ref[index, :, whole : whole + LANES] = tail
        real_ref[index, :, whole + LANES :] = ends
        return real_ref[index]

    def before(value):
        return pltpu.roll(value, 1, 1)

    def after(value):
        return pltpu.roll(value, padded - 1, 1)

    def face_y(f):
        face = 0.5 * (courant(row_ref[0, f]) + courant(row_ref[0, f + 1]))
        inside = jnp.logical_and(f >= least_face, f <= most_face)
        return up_and_down(face * jnp.where(inside, 1.0, 0.0))

    (rise_below, fall_below), (rise_above, fall_above) = face_y(j), face_y(j + 1)
    courant_x = extend(3 * (j % 2), courant(wind_ref[j].astype(jnp.float32)))
    rise_x, fall_x = up_and_down(0.5 * (before(courant_x) + courant_x))
    for i in range(2):
        below, here, above = (row_ref[1 + i, j + k] for k in range(3))
        field = extend(3 * (j % 2) + 1 + i, here)
        flux_x = rise_x * before(field) + fall_x * field
        across = rise_above * here + fall_above * above - rise_below * below - fall_below * here
        result = field - (after(flux_x) - flux_x)
        if i == 0:
            result = result - THICK_MID
        moved_ref[j, i * level_rows : (i + 1) * level_rows, :lon_count] = (
            result[:, :lon_count] - across
        )


def band_weights(index_ref, frac_ref, weight_ref):
    _, level_count, wide = weight_ref.shape

    def inner(k):
        return jnp.where(index_ref[k] == k, 1.0, frac_ref[k])

    def outer(k):
        return jnp.where(index_ref[k] == k, frac_ref[k], 0.0)

    def weigh(k):
        for place, weight in enumerate(
            (1.0 - inner(k), inner(k + 1) - outer(k), outer(k + 1))
        ):
            weight_ref[place, pl.ds(k, 1), :] = jnp.full((1, wide), weight, jnp.float32)

    loop(level_count, weigh)


def fold(wind, slot, slot_ref, work_ref, split_ref, rows):
    level_rows, lon_count = wind.shape
    padded = slot_ref.shape[2]
    parts, _ = filter_parts(lon_count)
    half, quarter, eighth = (part[2] for part in parts[:3])
    half_wide, quarter_wide, eighth_wide = (padded_to(part[2]) for part in parts[:3])
    slot_ref[slot, :, lon_count:] = jnp.zeros((level_rows, padded - lon_count), jnp.float32)
    slot_ref[slot, :, :lon_count] = wind
    near = slot_ref[slot, :, :half_wide]
    far = slot_ref[slot, :, half : half + half_wide]
    odd, even = near - far, near + far
    work_ref[slot, :, :half_wide] = even
    near = even[:, :quarter_wide]
    far = work_ref[slot, :, quarter : quarter + quarter_wide]
    two, even = near - far, near + far
    work_ref[slot, :, half_wide : half_wide + quarter_wide] = even
    near = even[:, :eighth_wide]
    far = work_ref[slot, :, half_wide + eighth : half_wide + eighth + eighth_wide]
    row = jnp.concatenate([odd, two, near - far, near + far], axis=1)
    high = row.astype(jnp.bfloat16).astype(jnp.float32)
    both = jnp.concatenate([high, row - high], axis=0)
    split_ref[rows, :] = both.astype(jnp.bfloat16)


def load(
    lat_count,
    index_hbm,
    frac_hbm,
    u_hbm,
    v_hbm,
    thick_hbm,
    tracer_hbm,
    table_hbm,
    damp_hbm,
    u_ref,
    v_ref,
    thick_ref,
    tracer_ref,
    table_ref,
    damp_ref,
    turned_ref,
    u_out,
    v_out,
    send_ref,
    split_ref,
    moved_ref,
    weight_ref,
    row_ref,
    real_ref,
    work_ref,
    index_ref,
    frac_ref,
    sems,
    table_sems,
):
    lat_rows, level_rows, lon_count = u_ref.shape
    f32 = jnp.float32
    polar = band_is_polar(lax.axis_index("lat") * lat_rows, lat_rows, lat_count)
    inputs = [
        pltpu.make_async_copy(source, target, sems.at[place])
        for place, (source, target) in enumerate(
            ((v_hbm, v_ref), (thick_hbm, thick_ref), (tracer_hbm, tracer_ref), (u_hbm, u_ref))
        )
    ]
    tables = [pltpu.make_async_copy(damp_hbm, damp_ref, sems.at[4])]
    parts, _ = filter_parts(lon_count)
    places = table_places(parts)
    points, split_at, columns = parts[0][2], places[0][2], table_hbm.shape[1]
    upper = places[2][0] + places[2][2]
    chunks = table_sems.shape[0] - 1
    height = upper // chunks

    def table_copy(chunk):
        if isinstance(chunk, int) and chunk == chunks:
            part = (pl.ds(upper, points - upper), pl.ds(0, split_at))
        else:
            part = (rows_at(chunk, height), pl.ds(0, columns))
        return pltpu.make_async_copy(
            table_hbm.at[part], table_ref.at[part], table_sems.at[chunk]
        )

    tables += [table_copy(chunk) for chunk in range(chunks + 1)]
    for copy in inputs:
        copy.start()

    @pl.when(polar)
    def _():
        for copy in tables:
            copy.start()

    scalars = [
        pltpu.make_async_copy(index_hbm, index_ref, sems.at[7]),
        pltpu.make_async_copy(frac_hbm, frac_ref, sems.at[8]),
    ]
    for copy in scalars:
        copy.start()

    def weigh():
        for copy in scalars:
            copy.wait()
        band_weights(index_ref, frac_ref, weight_ref)

    @pl.when(polar)
    def _():
        weigh()
        for copy in inputs:
            copy.wait()
        slots = real_ref.shape[0]
        for g in range(2 * lat_rows):
            wind = (u_ref if g < lat_rows else v_ref)[g % lat_rows].astype(f32)
            rows = slice(2 * level_rows * g, 2 * level_rows * (g + 1))
            fold(wind, g % slots, real_ref, work_ref, split_ref, rows)
        table_ref[points:split_at, :split_at] = jnp.zeros((split_at - points, split_at), jnp.bfloat16)
        for chunk in range(chunks + 1):
            table_copy(chunk).wait()
            start, stop = chunk * height, (chunk + 1) * height
            for top, left, size in places:
                low, high = max(start, top), min(stop, top + size)
                if low < high:
                    turned_ref[top : top + size, left + low - top : left + high - top] = (
                        table_ref[low:high, left : left + size].T
                    )
        tables[0].wait()

    @pl.when(jnp.logical_not(polar))
    def _():
        for copy in inputs:
            copy.wait()
        winds = [
            pltpu.make_async_copy(u_ref, u_out, sems.at[5]),
            pltpu.make_async_copy(v_ref, v_out, sems.at[6]),
        ]
        for copy in winds:
            copy.start()
        blank = jnp.zeros((level_rows, lon_count), f32)
        for place in range(3):
            row_ref[place, 0] = blank
            row_ref[place, lat_rows + 1] = blank

        def prepare(j):
            thick = thick_ref[j]
            row_ref[0, j + 1] = v_ref[j].astype(f32)
            row_ref[1, j + 1] = thick
            row_ref[2, j + 1] = tracer_ref[j] * thick

        loop(lat_rows, prepare)

        def advect(j):
            transport(j, u_ref, row_ref, real_ref, moved_ref, 1, lat_rows - 1)

            @pl.when(jnp.logical_and(j > 0, j < lat_rows - 1))
            def _():
                to_sectors(send_ref, moved_ref, j, lon_count // send_ref.shape[0])

        loop(lat_rows, advect, 2)
        weigh()
        for copy in winds:
            copy.wait()


def filter_advect(
    lat_count,
    u_ref,
    v_ref,
    thick_ref,
    tracer_ref,
    table_ref,
    damp_ref,
    turned_ref,
    partial_ref,
    next_ref,
    near_ref,
    u_held,
    v_held,
    send_held,
    split_held,
    u_hbm,
    v_hbm,
    send_ref,
    split_ref,
    u_out,
    v_out,
    real_ref,
    work_ref,
    prod_ref,
    spec_ref,
    row_ref,
    moved_ref,
    sems,
):
    lat_rows, level_rows, lon_count = u_ref.shape
    groups, _, padded = real_ref.shape
    distances = damp_ref.shape[0]
    first_lat = lax.axis_index("lat") * lat_rows
    f32 = jnp.float32
    bf16 = jnp.bfloat16
    parts, columns = filter_parts(lon_count)
    places = table_places(parts)
    odd_device = lax.axis_index("lat") % 2
    polar = band_is_polar(first_lat, lat_rows, lat_count)

    for side in range(2):
        for source, odd in ((near_ref, 1 - side), (next_ref, side)):

            @pl.when(odd_device == odd)
            def _():
                for place in range(3):
                    row_ref[place, side * (lat_rows + 1)] = source[place].astype(f32)

    @pl.when(jnp.logical_not(polar))
    def _():
        for side, j in enumerate((0, lat_rows - 1)):
            outer = side * (lat_rows + 1)
            own = courant(v_ref[j].astype(f32))
            face = 0.5 * (courant(row_ref[0, outer]) + own)
            at_pole = first_lat + side * lat_rows == side * lat_count
            rise, fall = up_and_down(face * jnp.where(at_pole, 0.0, 1.0))
            thick = thick_ref[j]
            for i, here in enumerate((thick, tracer_ref[j] * thick)):
                rows = slice(i * level_rows, (i + 1) * level_rows)
                if side:
                    value = partial_ref[j, rows, :lon_count] - (
                        rise * here + fall * row_ref[1 + i, outer]
                    )
                else:
                    value = partial_ref[j, rows, :lon_count] + (
                        rise * row_ref[1 + i, outer] + fall * here
                    )
                moved_ref[j, rows, :lon_count] = value
            to_sectors(send_ref, moved_ref, j, lon_count // send_ref.shape[0])

    @pl.when(polar)
    def _():
        def prepare(j):
            thick = thick_ref[j]
            row_ref[0, j + 1] = v_ref[j].astype(f32)
            row_ref[1, j + 1] = thick
            row_ref[2, j + 1] = tracer_ref[j] * thick
            u_out[j] = u_ref[j]
            v_out[j] = v_ref[j]

        loop(lat_rows, prepare)
        half, quarter, eighth = (part[2] for part in parts[:3])
        half_wide, quarter_wide, eighth_wide = (padded_to(part[2]) for part in parts[:3])

        def lat_of(g):
            if g < 2 * lat_rows:
                return first_lat + g % lat_rows
            return first_lat + (lat_rows if g % 2 else -1)

        for side in range(2):
            g = 2 * lat_rows + side
            rows = slice(2 * level_rows * g, 2 * level_rows * (g + 1))
            wind = row_ref[0, side * (lat_rows + 1)]
            fold(wind, side, real_ref, work_ref, split_ref, rows)

        for (_, _, _, column), (top, left, size) in zip(parts, places):
            prod_ref[:, column : column + size] = jnp.dot(
                split_ref[:, column : column + size],
                table_ref[top : top + size, left : left + size],
                preferred_element_type=f32,
            )

        for pair in range(groups // 2):
            values = []
            for g in (2 * pair, 2 * pair + 1):
                start = 2 * level_rows * g
                high = prod_ref[start : start + level_rows, :]
                low = prod_ref[start + level_rows : start + 2 * level_rows, :]
                place = jnp.clip(distance(lat_of(g), lat_count), 0, distances - 1)
                values.append((high + low) * damp_ref[place])
            spec_ref[2 * level_rows * pair : 2 * level_rows * (pair + 1), :] = jnp.concatenate(
                values, axis=0
            ).astype(bf16)
        rows = groups * level_rows

        for (_, _, _, column), (top, left, size) in zip(parts, places):
            prod_ref[:rows, column : column + size] = jnp.dot(
                spec_ref[:, column : column + size],
                turned_ref[top : top + size, left : left + size],
                preferred_element_type=f32,
            )

        for g in range(groups):
            start = level_rows * g
            odd, two, four, eight = (
                prod_ref[start : start + level_rows, column : column + padded_to(points)]
                for _, _, points, column in parts
            )
            work_ref[g, :, :eighth_wide] = eight + four
            work_ref[g, :, eighth : 2 * eighth] = (eight - four)[:, :eighth]
            even = work_ref[g, :, :quarter_wide]
            work_ref[g, :, :quarter_wide] = even + two
            work_ref[g, :, quarter : 2 * quarter] = (even - two)[:, :quarter]
            even = work_ref[g, :, :half_wide]
            scale = 1.0 / lon_count
            real_ref[g, :, :half_wide] = (even + odd) * scale
            real_ref[g, :, half : 2 * half] = ((even - odd) * scale)[:, :half]

        def finish(j):
            @pl.when(is_polar(first_lat + j, lat_count))
            def _():
                u_out[j] = real_ref[j, :, :lon_count].astype(bf16)
                smooth = real_ref[lat_rows + j, :, :lon_count].astype(bf16)
                v_out[j] = smooth
                row_ref[0, j + 1] = smooth.astype(f32)

        loop(lat_rows, finish)
        for side in range(2):

            @pl.when(is_polar(lat_of(2 * lat_rows + side), lat_count))
            def _():
                smooth = real_ref[2 * lat_rows + side, :, :lon_count].astype(bf16)
                row_ref[0, side * (lat_rows + 1)] = smooth.astype(f32)

        winds_out = [
            pltpu.make_async_copy(u_out, u_hbm, sems.at[0]),
            pltpu.make_async_copy(v_out, v_hbm, sems.at[1]),
        ]
        for copy in winds_out:
            copy.start()
        least = jnp.where(first_lat == 0, 1, 0)
        most = jnp.where(first_lat + lat_rows == lat_count, lat_rows - 1, lat_rows)

        def advect(j):
            transport(j, u_out, row_ref, real_ref, moved_ref, least, most)
            to_sectors(send_ref, moved_ref, j, lon_count // send_ref.shape[0])

        loop(lat_rows, advect, 2)
        for copy in winds_out:
            copy.wait()


def remap(weight_ref, recv_ref, thick_hbm, tracer_hbm, thick_out, tracer_out, sems):
    lat_rows, level_count, sector = thick_out.shape
    sources, _, wide = recv_ref.shape
    level_rows = level_count // sources
    f32 = jnp.float32
    below, here, above = (weight_ref[place] for place in range(3))
    place = lax.broadcasted_iota(jnp.int32, (level_rows, wide), 0)
    top, bottom = place == 0, place == level_rows - 1

    def results_out(j):
        return [
            pltpu.make_async_copy(source.at[j], target.at[j], sems.at[i, j])
            for i, (source, target) in enumerate(
                ((thick_out, thick_hbm), (tracer_out, tracer_hbm))
            )
        ]

    def work(j):
        blocks = [
            recv_ref[source, rows_at(j, 2 * level_rows), :].astype(f32)
            for source in range(sources)
        ]
        results = []
        for index in range(2):
            layers = [block[level_rows * index : level_rows * (index + 1)] for block in blocks]
            if index == 0:
                layers = [layer + THICK_MID for layer in layers]
            down = [pltpu.roll(layer, 1, 0) for layer in layers]
            up = [pltpu.roll(layer, level_rows - 1, 0) for layer in layers]
            outs = []
            for source in range(sources):
                chosen = slice(level_rows * source, level_rows * (source + 1))
                lower = jnp.where(top, down[max(source - 1, 0)], down[source])
                higher = jnp.where(bottom, up[min(source + 1, sources - 1)], up[source])
                outs.append(
                    below[chosen] * lower + here[chosen] * layers[source] + above[chosen] * higher
                )
            results.append(outs)
        for source in range(sources):
            chosen = slice(level_rows * source, level_rows * (source + 1))
            thick, mass = results[0][source], results[1][source]
            thick_out[j, chosen, :] = thick[:, :sector]
            tracer_out[j, chosen, :] = (mass / thick)[:, :sector]
        for copy in results_out(j):
            copy.start()

    loop(lat_rows, work)
    for j in range(lat_rows):
        for copy in results_out(j):
            copy.wait()


def per_device(u_wind, v_wind, thickness, tracer, remap_index, remap_frac):
    lat_rows, level_rows, lon_count = u_wind.shape
    lat_devices = lax.axis_size("lat")
    lat_count = lat_rows * lat_devices
    sectors = lax.axis_size("lev")
    level_count = level_rows * sectors
    sector = lon_count // sectors
    sector_wide = padded_to(sector)
    tables, damping = filter_tables(lat_count, lon_count)
    columns = damping.shape[2]
    padded = (lon_count // LANES + 2) * LANES
    f32, bf16 = jnp.float32, jnp.bfloat16

    in_hbm = pl.BlockSpec(memory_space=pltpu.HBM)
    in_vmem = pl.BlockSpec(memory_space=pltpu.VMEM)

    def limit(mebibytes):
        return pltpu.CompilerParams(vmem_limit_bytes=mebibytes * 1024 * 1024)

    edges = (3, level_rows, lon_count)

    def stay(array):
        return pltpu.with_memory_space_constraint(jnp.asarray(array), pltpu.HBM)

    near, beyond = pl.pallas_call(
        pack,
        out_shape=(pltpu.VMEM(edges, bf16), pltpu.VMEM(edges, bf16)),
        in_specs=[in_hbm] * 3,
        out_specs=(in_vmem, in_vmem),
        scratch_shapes=[
            pltpu.VMEM((2, level_rows, lon_count), bf16),
            pltpu.VMEM((2, level_rows, lon_count), f32),
            pltpu.VMEM((2, level_rows, lon_count), f32),
            pltpu.SemaphoreType.DMA((6,)),
        ],
        compiler_params=limit(8),
        name="pack",
    )(*(stay(array) for array in (v_wind, thickness, tracer)))
    swap_near = [(i, i ^ 1) for i in range(lat_devices)]
    swap_next = [(i, i - 1 + 2 * (i % 2)) for i in range(1, lat_devices - 1)]
    near = lax.ppermute(near, "lat", swap_near)
    beyond = lax.ppermute(beyond, "lat", swap_next)

    arrays = (u_wind, v_wind, thickness, tracer, tables, damping)
    moved_bytes = sum(array.size * array.dtype.itemsize for array in arrays)
    send_shape = (sectors, 2 * lat_rows * level_rows, sector_wide)
    moved_shape = (lat_rows, 2 * level_rows, padded)
    groups = 2 * lat_rows + 2
    held = (
        pltpu.HBM(u_wind.shape, bf16),
        pltpu.HBM(v_wind.shape, bf16),
        pltpu.VMEM(send_shape, bf16),
        pltpu.VMEM((2 * groups * level_rows, columns), bf16),
    )
    in_held = [in_hbm, in_hbm, in_vmem, in_vmem]
    rows_shape = (3, lat_rows + 2, level_rows, lon_count)
    *loaded, u_filtered, v_filtered, send, split, moved, weights = pl.pallas_call(
        functools.partial(load, lat_count),
        out_shape=[pltpu.VMEM(array.shape, array.dtype) for array in (*arrays, tables)]
        + [*held, pltpu.VMEM(moved_shape, f32), pltpu.VMEM((3, level_count, sector_wide), f32)],
        in_specs=[in_hbm] * (2 + len(arrays)),
        out_specs=[in_vmem] * (len(arrays) + 1) + in_held + [in_vmem] * 2,
        scratch_shapes=[
            pltpu.VMEM(rows_shape, f32),
            pltpu.VMEM((6, level_rows, padded), f32),
            pltpu.VMEM((6, level_rows, padded), f32),
            pltpu.SMEM(remap_index.shape, jnp.int32),
            pltpu.SMEM(remap_frac.shape, f32),
            pltpu.SemaphoreType.DMA((9,)),
            pltpu.SemaphoreType.DMA((4,)),
        ],
        compiler_params=limit(8),
        cost_estimate=pl.CostEstimate(flops=0, bytes_accessed=moved_bytes, transcendentals=0),
        name="load",
    )(*(stay(array) for array in (remap_index, remap_frac, *arrays)))
    before_held = len(loaded) + 3
    u_filtered, v_filtered, send, _ = pl.pallas_call(
        functools.partial(filter_advect, lat_count),
        out_shape=held,
        in_specs=[in_vmem] * before_held + in_held,
        out_specs=tuple(in_held),
        input_output_aliases={before_held + i: i for i in range(4)},
        scratch_shapes=[
            pltpu.VMEM(u_wind.shape, bf16),
            pltpu.VMEM(v_wind.shape, bf16),
            pltpu.VMEM((groups, level_rows, padded), f32),
            pltpu.VMEM((groups, level_rows, padded), f32),
            pltpu.VMEM((2 * groups * level_rows, columns), f32),
            pltpu.VMEM((groups * level_rows, columns), bf16),
            pltpu.VMEM(rows_shape, f32),
            pltpu.VMEM(moved_shape, f32),
            pltpu.SemaphoreType.DMA((2,)),
        ],
        compiler_params=limit(20),
        name="filter_advect",
    )(*loaded, moved, beyond, near, u_filtered, v_filtered, send, split)
    recv = lax.all_to_all(send, "lev", split_axis=0, concat_axis=0, tiled=True)
    shape = (lat_rows, level_count, sector)
    thick_out, tracer_out = pl.pallas_call(
        remap,
        out_shape=(pltpu.HBM(shape, f32), pltpu.HBM(shape, f32)),
        in_specs=[in_vmem] * 2,
        out_specs=(in_hbm, in_hbm),
        scratch_shapes=[
            pltpu.VMEM(shape, f32),
            pltpu.VMEM(shape, f32),
            pltpu.SemaphoreType.DMA((2, lat_rows)),
        ],
        compiler_params=limit(8),
        name="remap",
    )(weights, recv)
    return u_filtered, v_filtered, thick_out, tracer_out


def solution(mesh):
    placed = (
        P("lat", "lev", None),
        P("lat", "lev", None),
        P("lat", "lev", None),
        P("lat", "lev", None),
        P(),
        P(),
    )
    return jax.shard_map(
        per_device,
        mesh=mesh,
        in_specs=placed,
        out_specs=(
            P("lat", "lev", None),
            P("lat", "lev", None),
            P("lat", None, "lev"),
            P("lat", None, "lev"),
        ),
        check_vma=False,
    )
```

```python
import functools
import math

import jax
import jax.numpy as jnp
import ml_dtypes
import numpy as np
from jax import lax
from jax.experimental import pallas as pl
from jax.experimental.pallas import tpu as pltpu
from jax.sharding import PartitionSpec as P

COS_EDGE = math.cos(66.0 * math.pi / 180.0)
LANES = 128
THICK_MID = 1.0


def padded_to(count):
    return -(-count // LANES) * LANES


def filter_parts(lon_count):
    parts = []
    column = 0
    for first, step, points in (
        (1, 2, lon_count // 2),
        (2, 4, lon_count // 4),
        (4, 8, lon_count // 8),
        (0, 8, lon_count // 8),
    ):
        parts.append((first, step, points, column))
        column += padded_to(points)
    return parts, column


def table_places(parts):
    odd, two, four, eight = (padded_to(part[2]) for part in parts)
    return [(0, 0, odd), (0, odd, two), (two, odd, four), (two, odd + four, eight)]


def filter_tables(lat_count, lon_count):
    phase = 2.0 * np.pi * np.arange(lon_count) / lon_count
    rounded = (np.cos(phase) + np.sin(phase)).astype(np.float32).astype(ml_dtypes.bfloat16)
    polar = [d for d in range((lat_count + 1) // 2) if 15 * d < 2 * (lat_count - 1)]
    ratio = (np.sin(np.pi * np.array(polar, np.float64) / (lat_count - 1)) / COS_EDGE) ** 2
    wave = np.arange(lon_count)
    wave = np.minimum(wave, lon_count - wave)
    sine_square = np.sin(np.pi * wave / lon_count) ** 2
    sine_square[0] = 1.0
    values = np.minimum(1.0, ratio[:, None] / sine_square[None, :])
    values[:, 0] = 1.0

    parts, columns = filter_parts(lon_count)
    places = table_places(parts)
    tables = np.zeros((places[0][2], places[0][2] + places[1][2]), ml_dtypes.bfloat16)
    damping = np.zeros((len(polar), 1, columns), np.float32)
    for (first, step, points, column), (row, left, _) in zip(parts, places):
        waves = first + step * np.arange(points)
        values_here = rounded[np.arange(points)[:, None] * waves[None, :] % lon_count]
        tables[row : row + points, left : left + points] = values_here
        damping[:, 0, column : column + points] = values[:, waves]
    return tables, damping


def distance(lat, lat_count):
    return jnp.minimum(lat, lat_count - 1 - lat)


def is_polar(lat, lat_count):
    d = distance(lat, lat_count)
    return jnp.logical_and(d >= 0, 15 * d < 2 * (lat_count - 1))


def band_is_polar(first_lat, lat_rows, lat_count):
    found = is_polar(first_lat, lat_count)
    for offset in (-1, lat_rows - 1, lat_rows):
        found = jnp.logical_or(found, is_polar(first_lat + offset, lat_count))
    return found


def pack(v_hbm, thick_hbm, tracer_hbm, near_out, next_out, v_buf, thick_buf, tracer_buf, sems):
    lat_rows = v_hbm.shape[0]
    copies = []
    for side, row in enumerate((0, lat_rows - 1)):
        for source, target in ((v_hbm, v_buf), (thick_hbm, thick_buf), (tracer_hbm, tracer_buf)):
            copy = pltpu.make_async_copy(source.at[row], target.at[side], sems.at[len(copies)])
            copy.start()
            copies.append(copy)
    for copy in copies:
        copy.wait()
    odd = lax.axis_index("lat") % 2
    for out, side in ((near_out, 1 - odd), (next_out, odd)):
        thick = thick_buf[side]
        out[0] = v_buf[side]
        out[1] = thick.astype(jnp.bfloat16)
        out[2] = (tracer_buf[side] * thick).astype(jnp.bfloat16)


def courant(wind):
    return jnp.clip(0.05 * wind, -0.15, 0.15)


def loop(count, body, unroll=1):
    def step(place, carry):
        body(place)
        return carry

    lax.fori_loop(0, count, step, 0, unroll=unroll)


def rows_at(place, count):
    return pl.ds(pl.multiple_of(place * count, count), count)


def up_and_down(face):
    return jnp.maximum(face, 0.0), jnp.minimum(face, 0.0)


def to_sectors(send_ref, moved_ref, j, sector):
    sectors, _, sector_wide = send_ref.shape
    height = moved_ref.shape[1]
    for s in range(sectors):
        block = moved_ref[j, :, s * sector : s * sector + sector_wide]
        send_ref[s, rows_at(j, height), :] = block.astype(send_ref.dtype)


def transport(j, wind_ref, row_ref, real_ref, moved_ref, least_face, most_face):
    level_rows, lon_count = row_ref.shape[2:]
    padded = real_ref.shape[2]
    whole = lon_count // LANES * LANES
    rest = lon_count - whole
    lane = lax.broadcasted_iota(jnp.int32, (level_rows, LANES), 1)

    def extend(index, value):
        real_ref[index, :, :lon_count] = value
        tail = jnp.where(
            lane < rest,
            real_ref[index, :, whole : whole + LANES],
            pltpu.roll(real_ref[index, :, :LANES], rest, 1),
        )
        ends = pltpu.roll(tail, LANES - rest, 1)
        real_ref[index, :, whole : whole + LANES] = tail
        real_ref[index, :, whole + LANES :] = ends
        return real_ref[index]

    def before(value):
        return pltpu.roll(value, 1, 1)

    def after(value):
        return pltpu.roll(value, padded - 1, 1)

    def face_y(f):
        face = 0.5 * (courant(row_ref[0, f]) + courant(row_ref[0, f + 1]))
        inside = jnp.logical_and(f >= least_face, f <= most_face)
        return up_and_down(face * jnp.where(inside, 1.0, 0.0))

    (rise_below, fall_below), (rise_above, fall_above) = face_y(j), face_y(j + 1)
    courant_x = extend(3 * (j % 2), courant(wind_ref[j].astype(jnp.float32)))
    rise_x, fall_x = up_and_down(0.5 * (before(courant_x) + courant_x))
    for i in range(2):
        below, here, above = (row_ref[1 + i, j + k] for k in range(3))
        field = extend(3 * (j % 2) + 1 + i, here)
        flux_x = rise_x * before(field) + fall_x * field
        across = rise_above * here + fall_above * above - rise_below * below - fall_below * here
        result = field - (after(flux_x) - flux_x)
        if i == 0:
            result = result - THICK_MID
        moved_ref[j, i * level_rows : (i + 1) * level_rows, :lon_count] = (
            result[:, :lon_count] - across
        )


def band_weights(index_ref, frac_ref, weight_ref):
    _, level_count, wide = weight_ref.shape

    def inner(k):
        return jnp.where(index_ref[k] == k, 1.0, frac_ref[k])

    def outer(k):
        return jnp.where(index_ref[k] == k, frac_ref[k], 0.0)

    def weigh(k):
        for place, weight in enumerate(
            (1.0 - inner(k), inner(k + 1) - outer(k), outer(k + 1))
        ):
            weight_ref[place, pl.ds(k, 1), :] = jnp.full((1, wide), weight, jnp.float32)

    loop(level_count, weigh)


def fold(wind, slot, slot_ref, work_ref, split_ref, rows):
    level_rows, lon_count = wind.shape
    padded = slot_ref.shape[2]
    parts, _ = filter_parts(lon_count)
    half, quarter, eighth = (part[2] for part in parts[:3])
    half_wide, quarter_wide, eighth_wide = (padded_to(part[2]) for part in parts[:3])
    slot_ref[slot, :, lon_count:] = jnp.zeros((level_rows, padded - lon_count), jnp.float32)
    slot_ref[slot, :, :lon_count] = wind
    near = slot_ref[slot, :, :half_wide]
    far = slot_ref[slot, :, half : half + half_wide]
    odd, even = near - far, near + far
    work_ref[slot, :, :half_wide] = even
    near = even[:, :quarter_wide]
    far = work_ref[slot, :, quarter : quarter + quarter_wide]
    two, even = near - far, near + far
    work_ref[slot, :, half_wide : half_wide + quarter_wide] = even
    near = even[:, :eighth_wide]
    far = work_ref[slot, :, half_wide + eighth : half_wide + eighth + eighth_wide]
    row = jnp.concatenate([odd, two, near - far, near + far], axis=1)
    high = row.astype(jnp.bfloat16).astype(jnp.float32)
    both = jnp.concatenate([high, row - high], axis=0)
    split_ref[rows, :] = both.astype(jnp.bfloat16)


def load(
    lat_count,
    index_hbm,
    frac_hbm,
    u_hbm,
    v_hbm,
    thick_hbm,
    tracer_hbm,
    table_hbm,
    damp_hbm,
    u_ref,
    v_ref,
    thick_ref,
    tracer_ref,
    table_ref,
    damp_ref,
    turned_ref,
    u_out,
    v_out,
    send_ref,
    split_ref,
    moved_ref,
    weight_ref,
    row_ref,
    real_ref,
    work_ref,
    index_ref,
    frac_ref,
    sems,
    table_sems,
):
    lat_rows, level_rows, lon_count = u_ref.shape
    f32 = jnp.float32
    polar = band_is_polar(lax.axis_index("lat") * lat_rows, lat_rows, lat_count)
    inputs = [
        pltpu.make_async_copy(source, target, sems.at[place])
        for place, (source, target) in enumerate(
            ((v_hbm, v_ref), (thick_hbm, thick_ref), (tracer_hbm, tracer_ref), (u_hbm, u_ref))
        )
    ]
    tables = [pltpu.make_async_copy(damp_hbm, damp_ref, sems.at[4])]
    parts, _ = filter_parts(lon_count)
    places = table_places(parts)
    points, split_at, columns = parts[0][2], places[0][2], table_hbm.shape[1]
    upper = places[2][0] + places[2][2]
    chunks = table_sems.shape[0] - 1
    height = upper // chunks

    def table_copy(chunk):
        if isinstance(chunk, int) and chunk == chunks:
            part = (pl.ds(upper, points - upper), pl.ds(0, split_at))
        else:
            part = (rows_at(chunk, height), pl.ds(0, columns))
        return pltpu.make_async_copy(
            table_hbm.at[part], table_ref.at[part], table_sems.at[chunk]
        )

    tables += [table_copy(chunk) for chunk in range(chunks + 1)]
    for copy in inputs:
        copy.start()

    @pl.when(polar)
    def _():
        for copy in tables:
            copy.start()

    scalars = [
        pltpu.make_async_copy(index_hbm, index_ref, sems.at[7]),
        pltpu.make_async_copy(frac_hbm, frac_ref, sems.at[8]),
    ]
    for copy in scalars:
        copy.start()

    def weigh():
        for copy in scalars:
            copy.wait()
        band_weights(index_ref, frac_ref, weight_ref)

    @pl.when(polar)
    def _():
        weigh()
        for copy in inputs:
            copy.wait()
        slots = real_ref.shape[0]
        for g in range(2 * lat_rows):
            wind = (u_ref if g < lat_rows else v_ref)[g % lat_rows].astype(f32)
            rows = slice(2 * level_rows * g, 2 * level_rows * (g + 1))
            fold(wind, g % slots, real_ref, work_ref, split_ref, rows)
        table_ref[points:split_at, :split_at] = jnp.zeros((split_at - points, split_at), jnp.bfloat16)
        for chunk in range(chunks + 1):
            table_copy(chunk).wait()
            start, stop = chunk * height, (chunk + 1) * height
            for top, left, size in places:
                low, high = max(start, top), min(stop, top + size)
                if low < high:
                    turned_ref[top : top + size, left + low - top : left + high - top] = (
                        table_ref[low:high, left : left + size].T
                    )
        tables[0].wait()

    @pl.when(jnp.logical_not(polar))
    def _():
        weigh()
        for copy in inputs:
            copy.wait()
        winds = [
            pltpu.make_async_copy(u_ref, u_out, sems.at[5]),
            pltpu.make_async_copy(v_ref, v_out, sems.at[6]),
        ]
        for copy in winds:
            copy.start()
        blank = jnp.zeros((level_rows, lon_count), f32)
        for place in range(3):
            row_ref[place, 0] = blank
            row_ref[place, lat_rows + 1] = blank

        def prepare(j):
            thick = thick_ref[j]
            row_ref[0, j + 1] = v_ref[j].astype(f32)
            row_ref[1, j + 1] = thick
            row_ref[2, j + 1] = tracer_ref[j] * thick

        loop(lat_rows, prepare)

        def advect(j):
            transport(j, u_ref, row_ref, real_ref, moved_ref, 1, lat_rows - 1)

            @pl.when(jnp.logical_and(j > 0, j < lat_rows - 1))
            def _():
                to_sectors(send_ref, moved_ref, j, lon_count // send_ref.shape[0])

        loop(lat_rows, advect, 2)
        for copy in winds:
            copy.wait()


def filter_advect(
    lat_count,
    u_ref,
    v_ref,
    thick_ref,
    tracer_ref,
    table_ref,
    damp_ref,
    turned_ref,
    partial_ref,
    next_ref,
    near_ref,
    u_held,
    v_held,
    send_held,
    split_held,
    u_hbm,
    v_hbm,
    send_ref,
    split_ref,
    u_out,
    v_out,
    real_ref,
    work_ref,
    prod_ref,
    spec_ref,
    row_ref,
    moved_ref,
    sems,
):
    lat_rows, level_rows, lon_count = u_ref.shape
    groups, _, padded = real_ref.shape
    distances = damp_ref.shape[0]
    first_lat = lax.axis_index("lat") * lat_rows
    f32 = jnp.float32
    bf16 = jnp.bfloat16
    parts, columns = filter_parts(lon_count)
    places = table_places(parts)
    odd_device = lax.axis_index("lat") % 2
    polar = band_is_polar(first_lat, lat_rows, lat_count)

    for side in range(2):
        for source, odd in ((near_ref, 1 - side), (next_ref, side)):

            @pl.when(odd_device == odd)
            def _():
                for place in range(3):
                    row_ref[place, side * (lat_rows + 1)] = source[place].astype(f32)

    @pl.when(jnp.logical_not(polar))
    def _():
        for side, j in enumerate((0, lat_rows - 1)):
            outer = side * (lat_rows + 1)
            own = courant(v_ref[j].astype(f32))
            face = 0.5 * (courant(row_ref[0, outer]) + own)
            at_pole = first_lat + side * lat_rows == side * lat_count
            rise, fall = up_and_down(face * jnp.where(at_pole, 0.0, 1.0))
            thick = thick_ref[j]
            for i, here in enumerate((thick, tracer_ref[j] * thick)):
                rows = slice(i * level_rows, (i + 1) * level_rows)
                if side:
                    value = partial_ref[j, rows, :lon_count] - (
                        rise * here + fall * row_ref[1 + i, outer]
                    )
                else:
                    value = partial_ref[j, rows, :lon_count] + (
                        rise * row_ref[1 + i, outer] + fall * here
                    )
                moved_ref[j, rows, :lon_count] = value
            to_sectors(send_ref, moved_ref, j, lon_count // send_ref.shape[0])

    @pl.when(polar)
    def _():
        def prepare(j):
            thick = thick_ref[j]
            row_ref[0, j + 1] = v_ref[j].astype(f32)
            row_ref[1, j + 1] = thick
            row_ref[2, j + 1] = tracer_ref[j] * thick
            u_out[j] = u_ref[j]
            v_out[j] = v_ref[j]

        loop(lat_rows, prepare)
        half, quarter, eighth = (part[2] for part in parts[:3])
        half_wide, quarter_wide, eighth_wide = (padded_to(part[2]) for part in parts[:3])

        def lat_of(g):
            if g < 2 * lat_rows:
                return first_lat + g % lat_rows
            return first_lat + (lat_rows if g % 2 else -1)

        for side in range(2):
            g = 2 * lat_rows + side
            rows = slice(2 * level_rows * g, 2 * level_rows * (g + 1))
            wind = row_ref[0, side * (lat_rows + 1)]
            fold(wind, side, real_ref, work_ref, split_ref, rows)

        for (_, _, _, column), (top, left, size) in zip(parts, places):
            prod_ref[:, column : column + size] = jnp.dot(
                split_ref[:, column : column + size],
                table_ref[top : top + size, left : left + size],
                preferred_element_type=f32,
            )

        for pair in range(groups // 2):
            values = []
            for g in (2 * pair, 2 * pair + 1):
                start = 2 * level_rows * g
                high = prod_ref[start : start + level_rows, :]
                low = prod_ref[start + level_rows : start + 2 * level_rows, :]
                place = jnp.clip(distance(lat_of(g), lat_count), 0, distances - 1)
                values.append((high + low) * damp_ref[place])
            spec_ref[2 * level_rows * pair : 2 * level_rows * (pair + 1), :] = jnp.concatenate(
                values, axis=0
            ).astype(bf16)
        rows = groups * level_rows

        for (_, _, _, column), (top, left, size) in zip(parts, places):
            prod_ref[:rows, column : column + size] = jnp.dot(
                spec_ref[:, column : column + size],
                turned_ref[top : top + size, left : left + size],
                preferred_element_type=f32,
            )

        for g in range(groups):
            start = level_rows * g
            odd, two, four, eight = (
                prod_ref[start : start + level_rows, column : column + padded_to(points)]
                for _, _, points, column in parts
            )
            work_ref[g, :, :eighth_wide] = eight + four
            work_ref[g, :, eighth : 2 * eighth] = (eight - four)[:, :eighth]
            even = work_ref[g, :, :quarter_wide]
            work_ref[g, :, :quarter_wide] = even + two
            work_ref[g, :, quarter : 2 * quarter] = (even - two)[:, :quarter]
            even = work_ref[g, :, :half_wide]
            scale = 1.0 / lon_count
            real_ref[g, :, :half_wide] = (even + odd) * scale
            real_ref[g, :, half : 2 * half] = ((even - odd) * scale)[:, :half]

        def finish(j):
            @pl.when(is_polar(first_lat + j, lat_count))
            def _():
                u_out[j] = real_ref[j, :, :lon_count].astype(bf16)
                smooth = real_ref[lat_rows + j, :, :lon_count].astype(bf16)
                v_out[j] = smooth
                row_ref[0, j + 1] = smooth.astype(f32)

        loop(lat_rows, finish)
        for side in range(2):

            @pl.when(is_polar(lat_of(2 * lat_rows + side), lat_count))
            def _():
                smooth = real_ref[2 * lat_rows + side, :, :lon_count].astype(bf16)
                row_ref[0, side * (lat_rows + 1)] = smooth.astype(f32)

        winds_out = [
            pltpu.make_async_copy(u_out, u_hbm, sems.at[0]),
            pltpu.make_async_copy(v_out, v_hbm, sems.at[1]),
        ]
        for copy in winds_out:
            copy.start()
        least = jnp.where(first_lat == 0, 1, 0)
        most = jnp.where(first_lat + lat_rows == lat_count, lat_rows - 1, lat_rows)

        def advect(j):
            transport(j, u_out, row_ref, real_ref, moved_ref, least, most)
            to_sectors(send_ref, moved_ref, j, lon_count // send_ref.shape[0])

        loop(lat_rows, advect, 2)
        for copy in winds_out:
            copy.wait()


def remap(weight_ref, recv_ref, thick_hbm, tracer_hbm, thick_out, tracer_out, sems):
    lat_rows, level_count, sector = thick_out.shape
    sources, _, wide = recv_ref.shape
    level_rows = level_count // sources
    f32 = jnp.float32
    below, here, above = (weight_ref[place] for place in range(3))
    place = lax.broadcasted_iota(jnp.int32, (level_rows, wide), 0)
    top, bottom = place == 0, place == level_rows - 1

    def results_out(j):
        return [
            pltpu.make_async_copy(source.at[j], target.at[j], sems.at[i, j])
            for i, (source, target) in enumerate(
                ((thick_out, thick_hbm), (tracer_out, tracer_hbm))
            )
        ]

    def work(j):
        blocks = [
            recv_ref[source, rows_at(j, 2 * level_rows), :].astype(f32)
            for source in range(sources)
        ]
        results = []
        for index in range(2):
            layers = [block[level_rows * index : level_rows * (index + 1)] for block in blocks]
            if index == 0:
                layers = [layer + THICK_MID for layer in layers]
            down = [pltpu.roll(layer, 1, 0) for layer in layers]
            up = [pltpu.roll(layer, level_rows - 1, 0) for layer in layers]
            outs = []
            for source in range(sources):
                chosen = slice(level_rows * source, level_rows * (source + 1))
                lower = jnp.where(top, down[max(source - 1, 0)], down[source])
                higher = jnp.where(bottom, up[min(source + 1, sources - 1)], up[source])
                outs.append(
                    below[chosen] * lower + here[chosen] * layers[source] + above[chosen] * higher
                )
            results.append(outs)
        for source in range(sources):
            chosen = slice(level_rows * source, level_rows * (source + 1))
            thick, mass = results[0][source], results[1][source]
            thick_out[j, chosen, :] = thick[:, :sector]
            tracer_out[j, chosen, :] = (mass / thick)[:, :sector]
        for copy in results_out(j):
            copy.start()

    loop(lat_rows, work)
    for j in range(lat_rows):
        for copy in results_out(j):
            copy.wait()


def per_device(u_wind, v_wind, thickness, tracer, remap_index, remap_frac):
    lat_rows, level_rows, lon_count = u_wind.shape
    lat_devices = lax.axis_size("lat")
    lat_count = lat_rows * lat_devices
    sectors = lax.axis_size("lev")
    level_count = level_rows * sectors
    sector = lon_count // sectors
    sector_wide = padded_to(sector)
    tables, damping = filter_tables(lat_count, lon_count)
    columns = damping.shape[2]
    padded = (lon_count // LANES + 2) * LANES
    f32, bf16 = jnp.float32, jnp.bfloat16

    in_hbm = pl.BlockSpec(memory_space=pltpu.HBM)
    in_vmem = pl.BlockSpec(memory_space=pltpu.VMEM)

    def limit(mebibytes):
        return pltpu.CompilerParams(vmem_limit_bytes=mebibytes * 1024 * 1024)

    edges = (3, level_rows, lon_count)

    def stay(array):
        return pltpu.with_memory_space_constraint(jnp.asarray(array), pltpu.HBM)

    near, beyond = pl.pallas_call(
        pack,
        out_shape=(pltpu.VMEM(edges, bf16), pltpu.VMEM(edges, bf16)),
        in_specs=[in_hbm] * 3,
        out_specs=(in_vmem, in_vmem),
        scratch_shapes=[
            pltpu.VMEM((2, level_rows, lon_count), bf16),
            pltpu.VMEM((2, level_rows, lon_count), f32),
            pltpu.VMEM((2, level_rows, lon_count), f32),
            pltpu.SemaphoreType.DMA((6,)),
        ],
        compiler_params=limit(8),
        name="pack",
    )(*(stay(array) for array in (v_wind, thickness, tracer)))
    swap_near = [(i, i ^ 1) for i in range(lat_devices)]
    swap_next = [(i, i - 1 + 2 * (i % 2)) for i in range(1, lat_devices - 1)]
    near = lax.ppermute(near, "lat", swap_near)
    beyond = lax.ppermute(beyond, "lat", swap_next)

    arrays = (u_wind, v_wind, thickness, tracer, tables, damping)
    moved_bytes = sum(array.size * array.dtype.itemsize for array in arrays)
    send_shape = (sectors, 2 * lat_rows * level_rows, sector_wide)
    moved_shape = (lat_rows, 2 * level_rows, padded)
    groups = 2 * lat_rows + 2
    held = (
        pltpu.HBM(u_wind.shape, bf16),
        pltpu.HBM(v_wind.shape, bf16),
        pltpu.VMEM(send_shape, bf16),
        pltpu.VMEM((2 * groups * level_rows, columns), bf16),
    )
    in_held = [in_hbm, in_hbm, in_vmem, in_vmem]
    rows_shape = (3, lat_rows + 2, level_rows, lon_count)
    *loaded, u_filtered, v_filtered, send, split, moved, weights = pl.pallas_call(
        functools.partial(load, lat_count),
        out_shape=[pltpu.VMEM(array.shape, array.dtype) for array in (*arrays, tables)]
        + [*held, pltpu.VMEM(moved_shape, f32), pltpu.VMEM((3, level_count, sector_wide), f32)],
        in_specs=[in_hbm] * (2 + len(arrays)),
        out_specs=[in_vmem] * (len(arrays) + 1) + in_held + [in_vmem] * 2,
        scratch_shapes=[
            pltpu.VMEM(rows_shape, f32),
            pltpu.VMEM((6, level_rows, padded), f32),
            pltpu.VMEM((6, level_rows, padded), f32),
            pltpu.SMEM(remap_index.shape, jnp.int32),
            pltpu.SMEM(remap_frac.shape, f32),
            pltpu.SemaphoreType.DMA((9,)),
            pltpu.SemaphoreType.DMA((4,)),
        ],
        compiler_params=limit(8),
        cost_estimate=pl.CostEstimate(flops=0, bytes_accessed=moved_bytes, transcendentals=0),
        name="load",
    )(*(stay(array) for array in (remap_index, remap_frac, *arrays)))
    before_held = len(loaded) + 3
    u_filtered, v_filtered, send, _ = pl.pallas_call(
        functools.partial(filter_advect, lat_count),
        out_shape=held,
        in_specs=[in_vmem] * before_held + in_held,
        out_specs=tuple(in_held),
        input_output_aliases={before_held + i: i for i in range(4)},
        scratch_shapes=[
            pltpu.VMEM(u_wind.shape, bf16),
            pltpu.VMEM(v_wind.shape, bf16),
            pltpu.VMEM((groups, level_rows, padded), f32),
            pltpu.VMEM((groups, level_rows, padded), f32),
            pltpu.VMEM((2 * groups * level_rows, columns), f32),
            pltpu.VMEM((groups * level_rows, columns), bf16),
            pltpu.VMEM(rows_shape, f32),
            pltpu.VMEM(moved_shape, f32),
            pltpu.SemaphoreType.DMA((2,)),
        ],
        compiler_params=limit(20),
        name="filter_advect",
    )(*loaded, moved, beyond, near, u_filtered, v_filtered, send, split)
    recv = lax.all_to_all(send, "lev", split_axis=0, concat_axis=0, tiled=True)
    shape = (lat_rows, level_count, sector)
    thick_out, tracer_out = pl.pallas_call(
        remap,
        out_shape=(pltpu.HBM(shape, f32), pltpu.HBM(shape, f32)),
        in_specs=[in_vmem] * 2,
        out_specs=(in_hbm, in_hbm),
        scratch_shapes=[
            pltpu.VMEM(shape, f32),
            pltpu.VMEM(shape, f32),
            pltpu.SemaphoreType.DMA((2, lat_rows)),
        ],
        compiler_params=limit(8),
        name="remap",
    )(weights, recv)
    return u_filtered, v_filtered, thick_out, tracer_out


def solution(mesh):
    placed = (
        P("lat", "lev", None),
        P("lat", "lev", None),
        P("lat", "lev", None),
        P("lat", "lev", None),
        P(),
        P(),
    )
    return jax.shard_map(
        per_device,
        mesh=mesh,
        in_specs=placed,
        out_specs=(
            P("lat", "lev", None),
            P("lat", "lev", None),
            P("lat", None, "lev"),
            P("lat", None, "lev"),
        ),
        check_vma=False,
    )
```
